128 devices in a mesh: band: 32 (over y, x_lo, z), col: 4 (over x_hi, core).
Axes of the slice: x: 4 (x_hi: 2, x_lo: 2; x = x_hi * 2 + x_lo), y: 4, z: 4, core: 2. Of those that a mesh axis runs over, the one named last changes fastest.
Arguments:
- demand: float32 [131072, 16], P(('band', 'col')), may hold values from -16 to 16
- lead_periods: int32 [131072], P(('band', 'col')), may hold values from 1 to 4
- matrix_tiles: float32 [32, 4, 128, 128, 128], P('band', 'col'), may hold values from -0.125 to 0.125
- tile_pos: int32 [32, 4, 128], P('band', 'col'), may hold values from 0 to 8191, as said below
- cost_vector: float32 [131072], P(('band', 'col')), may hold values from 0.05 to 7
- primal_init: float32 [131072, 16], P(('band', 'col')), may hold values from 0 to 2
- dual_init: float32 [131072, 16], P(('band', 'col')), may hold values from -6 to 6
- weight_init: float32 [16], replicated, may hold values from 0.5 to 2
Outputs:
- primal: float32 [131072, 16], P(('band', 'col'))
- dual_vars: float32 [131072, 16], P(('band', 'col'))
- weight: float32 [16], replicated
The draws below stay inside these ranges and needn't reach their ends.
Inputs may be any that keep to these rules, and one draw needn't show every extreme that they name: `tile_pos`: within one period and column block the 128 entries are different; entry v places its tile at row tile v // 256 of that period and column tile v % (256) of that column block.
All inputs are finite; a program needn't handle non-finite values.
Results may differ from the reference program's by a relative error of at most 0.0003.
Values sent between devices are 32-bit elements; how exact they have to be, the bound alone decides.
A program may use at most 64 MiB of HBM per device.

```python
import math
import jax
import jax.numpy as jnp
from jax import lax

TILE = 128
PERIOD_ROWS = 4096
SCEN = 16
ITERS = 3
LEAD_MAX = 4
NT = 128
SUB = 8
SLOTS = 8192
ORDER = 131072
N_BAND = 32
N_COL = 4


def ramp_scales(key, count):
    position = jnp.arange(count, dtype=jnp.float32) / count
    ramp_factor = 1.0 + 2.0 * position
    rough_part = jnp.exp(jax.random.uniform(key, (count,), jnp.float32, jnp.log(0.3), jnp.log(3.0)))
    return ramp_factor * rough_part


def draw_demand(key, part):
    key_scale = jax.random.fold_in(key, 11)
    key_body = jax.random.fold_in(key, 12)
    scales = ramp_scales(key_scale, ORDER)[:, None]
    return 0.5 * scales * jax.random.truncated_normal(key_body, -3.0, 3.0, (ORDER, SCEN), jnp.float32)


def draw_cost_vector(key, part):
    key_scale = jax.random.fold_in(key, 21)
    scales = ramp_scales(key_scale, ORDER)
    return 0.5 * scales


def draw_tile_pos(key, part):
    key_list = jax.random.split(jax.random.fold_in(key, 31), N_BAND * N_COL)

    def one_device(device_key):
        return jax.random.permutation(device_key, SLOTS)[:NT].astype(jnp.int32)
    return jax.vmap(one_device)(key_list).reshape(N_BAND, N_COL, NT)


def plant(values, rng, least, high):
    longest = values.shape.index(max(values.shape))
    spots = []
    for shift in (0, 1):
        where = [jax.random.randint(jax.random.fold_in(rng, axis), (), 0, length) for axis, length in enumerate(values.shape)]
        where[longest] = (where[longest] + shift) % values.shape[longest]
        spots.append(tuple(where))
    return values.at[spots[0]].set(least).at[spots[1]].set(high)


def level_of(stream_key, shape, cuts, smallest, high):
    factor_of = 1.0
    for axis_at, parts in cuts:
        heights = jax.random.uniform(jax.random.fold_in(jax.random.fold_in(stream_key, 6), axis_at), (parts,), jnp.float32, smallest / len(cuts), high / len(cuts))
        factor_of = factor_of * jnp.repeat(jnp.exp(heights), shape[axis_at] // parts).reshape((-1,) + (1,) * (len(shape) - 1 - axis_at))
    return factor_of


def gaussian(rng, shape, width, limit, pieces=(), held_as=jnp.bfloat16):
    level = level_of(rng, shape, pieces, -0.22, 0.18) if pieces else 1.0
    array = jax.random.normal(rng, shape, jnp.float32) * width * level
    return jnp.minimum(jnp.maximum(array, -limit), limit).astype(held_as)


def setup_inputs(seed: int = 0) -> dict:
    key_of = jax.random.split(jax.random.key(seed), 9)
    return {
        "demand": draw_demand(jax.random.fold_in(key_of[8], 71), 0),
        "lead_periods": plant(jax.random.randint(key_of[1], (ORDER,), 1, LEAD_MAX + 1), jax.random.fold_in(key_of[1], 1), 1, LEAD_MAX).astype(jnp.int32),
        "matrix_tiles": gaussian(key_of[2], (N_BAND, N_COL, NT, TILE, TILE), (NT * TILE // SUB) ** -0.5, 0.125, ((0, 32), (1, 4)), jnp.float32),
        "tile_pos": draw_tile_pos(jax.random.fold_in(key_of[8], 71), 0),
        "cost_vector": draw_cost_vector(jax.random.fold_in(key_of[8], 71), 0),
        "primal_init": jnp.clip(2.0 * jax.random.uniform(key_of[5], (ORDER, SCEN), jnp.float32) ** level_of(key_of[5], (ORDER, SCEN), ((0, 128),), -0.2, 0.2), 0.0, 2.0),
        "dual_init": gaussian(key_of[6], (ORDER, SCEN), 1.0, 6.0, ((0, 128),), jnp.float32),
        "weight_init": jnp.clip(jnp.exp(jax.random.uniform(key_of[7], (SCEN,), jnp.float32, math.log(0.5), math.log(2.0))), 0.5, 2.0),
    }


step_scale = 0.45
return_share = 0.6
epsilon = 1e-06
highest = lax.Precision.HIGHEST

def apply_matrix(matrix_tiles, tile_pos, field):
    units_col = N_BAND * SUB
    units_row = N_COL * SUB
    field_grid = field.reshape(N_BAND, N_COL, SUB, TILE, SCEN)
    col_units = jnp.transpose(field_grid, (1, 0, 2, 3, 4)).reshape(N_COL, units_col, TILE, SCEN)
    column_ids = jnp.arange(N_COL, dtype=jnp.int32)[:, None]

    def one_band(inputs):
        band_tiles, band_pos = inputs
        picked = col_units[column_ids, band_pos % units_col]
        product = jnp.einsum('qtij,qtjs->qtis', band_tiles, picked, precision=highest)
        onehot = (band_pos[:, :, None] // units_col == jnp.arange(units_row, dtype=jnp.int32)[None, None, :]).astype(jnp.float32)
        return jnp.einsum('qtr,qtis->ris', onehot, product, precision=highest)
    result = lax.map(one_band, (matrix_tiles, tile_pos))
    return result.reshape(ORDER, SCEN)

def apply_transpose(matrix_tiles, tile_pos, dual_vars):
    units_col = N_BAND * SUB
    units_row = N_COL * SUB
    dual_grid = dual_vars.reshape(N_BAND, units_row, TILE, SCEN)
    column_ids = jnp.arange(N_COL, dtype=jnp.int32)[:, None]

    def one_band(running, inputs):
        band_tiles, band_pos, band_dual = inputs
        picked = band_dual[band_pos // units_col]
        product = jnp.einsum('qtij,qtis->qtjs', band_tiles, picked, precision=highest)
        running = running.at[column_ids, band_pos % units_col].add(product)
        return (running, None)
    start = jnp.zeros((N_COL, units_col, TILE, SCEN), jnp.float32)
    running, unused = lax.scan(one_band, start, (matrix_tiles, tile_pos, dual_grid))
    running = running.reshape(N_COL, N_BAND, SUB, TILE, SCEN)
    return jnp.transpose(running, (1, 0, 2, 3, 4)).reshape(ORDER, SCEN)

def reference(demand, lead_periods, matrix_tiles, tile_pos, cost_vector, primal_init, dual_init, weight_init):
    demand_grid = demand.reshape(N_BAND, PERIOD_ROWS, SCEN)
    lead_grid = lead_periods.reshape(N_BAND, PERIOD_ROWS, 1)
    lagged = jnp.zeros((N_BAND, PERIOD_ROWS, SCEN), jnp.float32)
    for lead in range(1, LEAD_MAX + 1):
        lagged = jnp.where(lead_grid == lead, jnp.roll(demand_grid, lead, axis=0), lagged)
    right_side = (demand_grid - return_share * lagged).reshape(ORDER, SCEN)
    primal = primal_init
    dual_vars = dual_init
    weight = weight_init
    for iteration in range(ITERS):
        primal_step = step_scale / weight
        dual_step = step_scale * weight
        pull_terms = apply_transpose(matrix_tiles, tile_pos, dual_vars)
        primal_new = jnp.maximum(primal - primal_step[None, :] * (cost_vector[:, None] - pull_terms), 0.0)
        push_terms = apply_matrix(matrix_tiles, tile_pos, 2.0 * primal_new - primal)
        dual_new = dual_vars + dual_step[None, :] * (right_side - push_terms)
        primal_change = primal_new - primal
        dual_change = dual_new - dual_vars
        primal_square = lax.optimization_barrier(jnp.sum(primal_change * primal_change, axis=0))
        dual_square = lax.optimization_barrier(jnp.sum(dual_change * dual_change, axis=0))
        weight = jnp.sqrt(weight * jnp.sqrt((primal_square + epsilon) / (dual_square + epsilon)))
        primal = primal_new
        dual_vars = dual_new
    return (primal, dual_vars, weight)
```

```python
import jax
import jax.numpy as jnp
from jax import lax
from jax.experimental import pallas as pl
from jax.experimental.pallas import tpu as pltpu
from jax.sharding import PartitionSpec as P

ITERS = 3
LEAD_MAX = 4
step_scale = 0.45
return_share = 0.6
epsilon = 1e-06

NT = 128
T = 128
CT = 256
RT = 32
F32 = jnp.float32
BF16 = jnp.bfloat16
CHUNKS = 16
MESH = pl.DeviceIdType.MESH

O_ROW, O_C0, O_C1, O_PC, O_PR = 0, 128, 256, 384, 512
O_L0, O_L1, O_LR = 640, 896, 1152
TABLE = 1184


def index_table(pos):
    pos = pos.reshape(-1)
    t = jnp.arange(NT, dtype=jnp.int32)
    row, col = pos // CT, pos % CT

    def order(c):
        k, z, x, y = c % 8, (c // 8) % 4, (c // 32) % 2, c // 64
        return ((z * 4 + y) * 2 + x) * 8 + k, ((y * 4 + z) * 2 + x) * 8 + k

    def prev(key):
        same = (key[:, None] == key[None, :]) & (t[:, None] < t[None, :])
        found = jnp.max(jnp.where(same, t[:, None], -1), axis=0)
        return jnp.where(found < 0, NT, found)

    def last(key, count):
        ids = jnp.arange(count, dtype=jnp.int32)
        found = jnp.max(jnp.where(key[:, None] == ids[None, :], t[:, None], -1), axis=0)
        return jnp.where(found < 0, NT, found)

    c0, c1 = order(col)
    drow = (row // 8) * 10 + row % 8
    return jnp.concatenate(
        [drow, c0, c1, prev(col), prev(row), last(c0, CT), last(c1, CT), last(row, RT)]
    )


def split(v):
    hi = v.astype(BF16).astype(F32)
    return hi, v - hi


class Copies:
    def __init__(self, make, count):
        self.make, self.count = make, count

    def __getitem__(self, i):
        return self.make(i)


def kernel(
    tab, dem, lead, a_hbm, cost, prim0, dual0, w0,
    prim_out, dual_out, w_out,
    af, wt, s_buf, xg0, xg1, pb, fb, rb, qb, tb, dg0, dg1, yb, cr, pr, rhs, lag, wgt, fs, fc, fz, fp,
    a_sem, lag_s, lag_r, ca_s, ca_r, rz_s, rz_r, rp_s, rp_r, ap_s, ap_r, az_s, az_r, cs_s, cs_r, fi_s, fi_r,
):
    b = lax.axis_index("band")
    q = lax.axis_index("col")
    y, x, z = b // 8, (b // 4) % 2, b % 4

    def rc(src, dst, ss, rs, band, col):
        return pltpu.make_async_remote_copy(
            src_ref=src, dst_ref=dst, send_sem=ss, recv_sem=rs,
            device_id=(band, col), device_id_type=MESH,
        )

    xg, dg = (xg0, xg1), (dg0, dg1)

    g_of = (z, y)
    m_of = (y * 2 + x, z * 2 + x)

    def band_of(h, g, m):
        o, xx = m // 2, m % 2
        return o * 8 + xx * 4 + g if h == 0 else g * 8 + xx * 4 + o

    def a_copy(i):
        n = NT // CHUNKS
        return pltpu.make_async_copy(a_hbm.at[pl.ds(i * n, n)], af.at[pl.ds(i * n, n)], a_sem.at[i])

    def lag_copy(l):
        return rc(dem, lag.at[l - 1], lag_s.at[l - 1], lag_r.at[l - 1], (b + l) % 32, q)

    def ca_copy(h, j):
        own = dg[h].at[pl.ds(q * 10, 10)]
        return rc(own, own, ca_s.at[h, j - 1], ca_r.at[h, j - 1], b, (q + j) % 4)

    def ca_recv(h, j):
        slot = dg[h].at[pl.ds(((q + 4 - j) % 4) * 10, 10)]
        return rc(slot, slot, ca_s.at[h, j - 1], ca_r.at[h, j - 1], b, (q + 4 - j) % 4)

    def ring(h):
        g = g_of[h]
        return g, (g + 1) % 4, (g + 3) % 4, (g + 2) % 4

    def rz_copies(h):
        g, up, dn, opp = ring(h)
        m = m_of[h]
        bu, bd = band_of(h, up, m), band_of(h, dn, m)

        def piece(block, half):
            return pb.at[h, pl.ds(block * 66 + (34 if half else 0), 32 if half else 34)]

        spec = (
            (piece(opp, 0), fb.at[h, 0], bu),
            (piece(opp, 1), fb.at[h, 1, pl.ds(0, 32)], bd),
            (piece(up, 1), rb.at[h, 0, pl.ds(34, 32)], bu),
            (piece(dn, 0), rb.at[h, 1, pl.ds(0, 34)], bd),
            (piece(up, 0), rb.at[h, 0, pl.ds(0, 34)], bu),
            (piece(dn, 1), rb.at[h, 1, pl.ds(34, 32)], bd),
        )
        return Copies(
            lambda i: rc(spec[i][0], spec[i][1], rz_s.at[h, i], rz_r.at[h, i], spec[i][2], q), 6
        )

    def rp_copy(h, j):
        m2 = (m_of[h] + j) % 8
        return rc(
            qb.at[h, m2], tb.at[h, j - 1], rp_s.at[h, j - 1], rp_r.at[h, j - 1], band_of(h, g_of[h], m2), q
        )

    def ap_copy(h, j, back=False):
        m = m_of[h]
        m2 = (m + 8 - j) % 8 if back else (m + j) % 8
        slot = xg[h].at[pl.ds((g_of[h] * 8 + (m2 if back else m)) * 8, 8)]
        return rc(slot, slot, ap_s.at[h, j - 1], ap_r.at[h, j - 1], band_of(h, g_of[h], m2), q)

    def az_copies(h, back=False):
        g, up, dn, opp = ring(h)
        m = m_of[h]
        bu, bd = band_of(h, up, m), band_of(h, dn, m)

        def piece(block, half):
            return xg[h].at[pl.ds(block * 64 + half * 32, 32)]

        lo, hi = (dn, up) if back else (g, g)
        spec = (
            (piece(lo, 0), bu),
            (piece(hi, 1), bd),
            (piece(lo, 1), bu),
            (piece(hi, 0), bd),
            (piece(opp if back else dn, 0), bu),
            (piece(opp if back else up, 1), bd),
        )
        return Copies(
            lambda i: rc(spec[i][0], spec[i][0], az_s.at[h, i], az_r.at[h, i], spec[i][1], q), 6
        )

    def cs_copy(h, j):
        q2 = (q + j) % 4
        return rc(yb.at[h, pl.ds(q2 * 8, 8)], cr.at[h, j - 1], cs_s.at[h, j - 1], cs_r.at[h, j - 1], b, q2)

    for i in range(CHUNKS):
        a_copy(i).start()
    zero = jnp.zeros((8, T), F32)
    for h in range(2):
        for k in range(8):
            dg[h][q * 10 + k] = dual0[8 * h:8 * h + 8, k * T:(k + 1) * T]
            pr[h, k] = prim0[8 * h:8 * h + 8, k * T:(k + 1) * T]
        dg[h][q * 10 + 8] = zero
        dg[h][q * 10 + 9] = zero
        wgt[h] = w0[8 * h:8 * h + 8, :]
        for j in (2, 1, 3):
            ca_copy(h, j).start()
    for l in range(1, LEAD_MAX + 1):
        lag_copy(l).start()
    s_buf[NT] = zero

    for i in range(CHUNKS):
        a_copy(i).wait()
        n = NT // CHUNKS

        def prep(t, carry):
            v = af[t]
            hi = v.astype(BF16)
            wt[t, 0] = hi
            wt[t, 1] = (v - hi.astype(F32)).astype(BF16)
            return carry

        lax.fori_loop(i * n, (i + 1) * n, prep, 0, unroll=2)

    def products(h, src, o_src, o_prev, forward):
        def pair(p, carry):
            t1, t2 = 2 * p, 2 * p + 1
            v1 = src[h][tab[o_src + t1]]
            v2 = src[h][tab[o_src + t2]]
            lhs = jnp.concatenate([*split(v1), *split(v2)], axis=0).astype(BF16)
            lhs = jnp.concatenate([lhs, lhs], axis=1)
            h1, l1, h2, l2 = wt[t1, 0], wt[t1, 1], wt[t2, 0], wt[t2, 1]
            if forward:
                w = jnp.concatenate(
                    [jnp.concatenate([h1, l1], axis=1), jnp.concatenate([h2, l2], axis=1)], axis=0
                )
                dims = (((1,), (1,)), ((), ()))
            else:
                w = jnp.concatenate(
                    [jnp.concatenate([h1, h2], axis=1), jnp.concatenate([l1, l2], axis=1)], axis=0
                )
                dims = (((1,), (0,)), ((), ()))
            out = lax.dot_general(lhs, w, dims, preferred_element_type=F32)
            s_buf[t1] = out[0:8, :T] + out[8:16, :T] + s_buf[tab[o_prev + t1]]
            s_buf[t2] = out[16:24, T:] + out[24:32, T:] + s_buf[tab[o_prev + t2]]
            return carry

        lax.fori_loop(0, NT // 2, pair, 0, unroll=4)

    def iteration(it, carry):
        for h in range(2):
            for j in range(1, 4):
                ca_recv(h, j).wait_recv()
            products(h, dg, O_ROW, O_PC, False)
            stat = [sum(dg[h][c * 10 + 8 + e] for c in range(4)) for e in range(2)]
            for g in range(4):
                pb[h, g * 66] = stat[0]
                pb[h, g * 66 + 1] = stat[1]

                def place(i, carry, g=g):
                    pb[h, g * 66 + 2 + i] = s_buf[tab[(O_L0, O_L1)[h] + g * 64 + i]]
                    return carry

                lax.fori_loop(0, 64, place, 0, unroll=8)
            copies = rz_copies(h)
            for i in range(4):
                copies[i].start()
        for h in range(2):
            g, up, dn, opp = ring(h)
            copies = rz_copies(h)
            copies[0].wait_recv()
            here = pl.ds(up * 66, 34)
            pb[h, here] = pb[h, here] + fb[h, 0]
            copies[4].start()
            copies[1].wait_recv()
            here = pl.ds(dn * 66 + 34, 32)
            pb[h, here] = pb[h, here] + fb[h, 1, 0:32]
            copies[5].start()
        for h in range(2):
            g = g_of[h]
            copies = rz_copies(h)
            for i in (2, 3, 4, 5):
                copies[i].wait_recv()
            stat = [pb[h, g * 66 + e] + rb[h, 0, e] + rb[h, 1, e] for e in range(2)]
            for m in range(8):
                for k in range(8):
                    i = 2 + m * 8 + k
                    qb[h, m, k] = pb[h, g * 66 + i] + rb[h, 0, i] + rb[h, 1, i]
                for e in range(2):
                    qb[h, m, 8 + e] = stat[e]
            for j in (4, 3, 5, 2, 6, 1, 7):
                rp_copy(h, j).start()
        for h in range(2):
            m = m_of[h]
            for j in range(1, 8):
                rp_copy(h, j).wait_recv()

            def total(k):
                return qb[h, m, k] + sum(tb[h, j, k] for j in range(7))

            psq = jnp.sum(total(8), axis=1, keepdims=True)
            dsq = jnp.sum(total(9), axis=1, keepdims=True)
            ratio = jnp.sqrt((psq + epsilon) / (dsq + epsilon))
            old = wgt[h]
            weight = jnp.where(it > 0, jnp.sqrt(old * ratio), old)
            wgt[h] = weight
            pstep = step_scale / weight
            square = jnp.zeros((8, T), F32)
            for k in range(8):
                primal = pr[h, k]
                new = jnp.maximum(primal - pstep * (cost[k:k + 1, :] - total(k)), 0.0)
                change = new - primal
                square = square + change * change
                pr[h, k] = new
                xg[h][(g_of[h] * 8 + m) * 8 + k] = 2.0 * new - primal
            for j in range(1, 4):
                ca_copy(h, j).wait_send()
            dg[h][q * 10 + 8] = square
            for j in (4, 3, 5, 2, 6, 1, 7):
                ap_copy(h, j).start()
        for h in range(2):
            for j in range(1, 8):
                ap_copy(h, j, True).wait_recv()
            copies = az_copies(h)
            for i in range(4):
                copies[i].start()
        for h in range(2):
            back, copies = az_copies(h, True), az_copies(h)
            back[0].wait_recv()
            copies[4].start()
            back[1].wait_recv()
            copies[5].start()

        @pl.when(it == 0)
        def _():
            for l in range(1, LEAD_MAX + 1):
                lag_copy(l).wait_recv()
            for h in range(2):
                rows = slice(8 * h, 8 * h + 8)
                for k in range(8):
                    lanes = slice(k * T, (k + 1) * T)
                    periods = jnp.broadcast_to(lead[k:k + 1, :], (8, T))
                    lagged = jnp.zeros((8, T), F32)
                    for l in range(1, LEAD_MAX + 1):
                        lagged = jnp.where(periods == l, lag[l - 1, rows, lanes], lagged)
                    rhs[h, k] = dem[rows, lanes] - return_share * lagged
            for l in range(1, LEAD_MAX + 1):
                lag_copy(l).wait_send()

        for h in range(2):
            back = az_copies(h, True)
            for i in (2, 3, 4, 5):
                back[i].wait_recv()
            products(h, xg, (O_C0, O_C1)[h], O_PR, True)
            for r in range(RT):
                yb[h, r] = s_buf[tab[O_LR + r]]
            for j in (2, 1, 3):
                cs_copy(h, j).start()
        for h in range(2):
            for j in range(1, 4):
                cs_copy(h, j).wait_recv()
            dstep = step_scale * wgt[h]
            square = jnp.zeros((8, T), F32)
            for k in range(8):
                push = yb[h, q * 8 + k] + (cr[h, 0, k] + cr[h, 1, k] + cr[h, 2, k])
                old = dg[h][q * 10 + k]
                new = old + dstep * (rhs[h, k] - push)
                change = new - old
                square = square + change * change
                dg[h][q * 10 + k] = new
            dg[h][q * 10 + 9] = square

            @pl.when(it < ITERS - 1)
            def _():
                for j in (2, 1, 3):
                    ca_copy(h, j).start()

        for h in range(2):
            for copies in (rz_copies(h), az_copies(h)):
                for i in range(6):
                    copies[i].wait_send()
            for j in range(1, 8):
                rp_copy(h, j).wait_send()
                ap_copy(h, j).wait_send()
            for j in range(1, 4):
                cs_copy(h, j).wait_send()
        return carry

    lax.fori_loop(0, ITERS, iteration, 0)

    for h in range(2):
        for e in range(2):
            fs[0, 2 * h + e] = dg[h][q * 10 + 8 + e]

    def fi_group(stage):
        if stage == 0:
            return [(b, (q + j) % 4) for j in range(1, 4)], fc, 0
        if stage == 1:
            return [(band_of(0, (z + j) % 4, m_of[0]), q) for j in range(1, 4)], fz, 3
        return [(band_of(0, z, (m_of[0] + j) % 8), q) for j in range(1, 8)], fp, 6

    def fi_copies(stage):
        group, dst, at = fi_group(stage)
        return [
            rc(fs.at[stage], dst.at[i], fi_s.at[at + i], fi_r.at[at + i], *to) for i, to in enumerate(group)
        ]

    for stage in range(3):
        copies = fi_copies(stage)
        for c in copies:
            c.start()
        if stage == 0:
            for h in range(2):
                for k in range(8):
                    prim_out[8 * h:8 * h + 8, k * T:(k + 1) * T] = pr[h, k]
                    dual_out[8 * h:8 * h + 8, k * T:(k + 1) * T] = dg[h][q * 10 + k]
        for c in copies:
            c.wait_recv()
        dst = fi_group(stage)[1]
        fs[stage + 1] = fs[stage] + sum(dst[i] for i in range(len(copies)))
    for h in range(2):
        psq = jnp.sum(fs[3, 2 * h], axis=1, keepdims=True)
        dsq = jnp.sum(fs[3, 2 * h + 1], axis=1, keepdims=True)
        ratio = jnp.sqrt((psq + epsilon) / (dsq + epsilon))
        w_out[8 * h:8 * h + 8, :] = jnp.sqrt(wgt[h] * ratio)
    for stage in range(3):
        for c in fi_copies(stage):
            c.wait_send()


def on_device(
    demand, lead_periods, matrix_tiles, tile_pos, cost_vector, primal_init, dual_init, weight_init
):
    table = index_table(tile_pos)
    vmem = pl.BlockSpec(memory_space=pltpu.VMEM)
    dma = pltpu.SemaphoreType.DMA

    def buf(*shape, dtype=F32):
        return pltpu.VMEM(shape, dtype)

    primal, dual, weight = pl.pallas_call(
        kernel,
        out_shape=(
            jax.ShapeDtypeStruct((16, 1024), F32),
            jax.ShapeDtypeStruct((16, 1024), F32),
            jax.ShapeDtypeStruct((16, T), F32),
        ),
        in_specs=[
            pl.BlockSpec(memory_space=pltpu.SMEM), vmem, vmem, pl.BlockSpec(memory_space=pl.ANY),
            vmem, vmem, vmem, vmem,
        ],
        out_specs=(vmem, vmem, vmem),
        scratch_shapes=[
            buf(NT, T, T),
            buf(NT, 2, T, T, dtype=BF16),
            buf(NT + 1, 8, T),
            buf(CT, 8, T),
            buf(CT, 8, T),
            buf(2, 264, 8, T),
            buf(2, 2, 34, 8, T),
            buf(2, 2, 66, 8, T),
            buf(2, 8, 10, 8, T),
            buf(2, 7, 10, 8, T),
            buf(40, 8, T),
            buf(40, 8, T),
            buf(2, RT, 8, T),
            buf(2, 3, 8, 8, T),
            buf(2, 8, 8, T),
            buf(2, 8, 8, T),
            buf(4, 16, 1024),
            buf(2, 8, T),
            buf(4, 4, 8, T),
            buf(3, 4, 8, T),
            buf(3, 4, 8, T),
            buf(7, 4, 8, T),
            dma((CHUNKS,)), dma((4,)), dma((4,)),
            dma((2, 3)), dma((2, 3)), dma((2, 6)), dma((2, 6)), dma((2, 7)), dma((2, 7)),
            dma((2, 7)), dma((2, 7)), dma((2, 6)), dma((2, 6)), dma((2, 3)), dma((2, 3)),
            dma((13,)), dma((13,)),
        ],
        compiler_params=pltpu.CompilerParams(
            has_side_effects=True, vmem_limit_bytes=48 * 2**20
        ),
    )(
        table,
        demand.T,
        lead_periods.reshape(8, T),
        matrix_tiles.reshape(NT, T, T),
        cost_vector.reshape(8, T),
        primal_init.T,
        dual_init.T,
        jnp.broadcast_to(weight_init[:, None], (16, T)),
    )
    return primal.T, dual.T, weight[:, 0]


def solution(mesh):
    in_specs = (
        P(("band", "col"), None),
        P(("band", "col")),
        P("band", "col", None, None, None),
        P("band", "col", None),
        P(("band", "col")),
        P(("band", "col"), None),
        P(("band", "col"), None),
        P(),
    )
    out_specs = (P(("band", "col"), None), P(("band", "col"), None), P())
    return jax.shard_map(
        on_device, mesh=mesh, in_specs=in_specs, out_specs=out_specs, check_vma=False
    )
```

```python
import jax
import jax.numpy as jnp
from jax import lax
from jax.experimental import pallas as pl
from jax.experimental.pallas import tpu as pltpu
from jax.sharding import PartitionSpec as P

ITERS = 3
LEAD_MAX = 4
step_scale = 0.45
return_share = 0.6
epsilon = 1e-06

NT = 128
T = 128
CT = 256
RT = 32
F32 = jnp.float32
BF16 = jnp.bfloat16
CHUNKS = 16
MESH = pl.DeviceIdType.MESH

O_ROW, O_C0, O_C1, O_PC, O_PR = 0, 128, 256, 384, 512
O_L0, O_L1, O_LR = 640, 896, 1152
TABLE = 1184


def index_table(pos):
    pos = pos.reshape(-1)
    t = jnp.arange(NT, dtype=jnp.int32)
    row, col = pos // CT, pos % CT

    def order(c):
        k, z, x, y = c % 8, (c // 8) % 4, (c // 32) % 2, c // 64
        chunk, kk = k // 4, k % 4
        return (((z * 2 + chunk) * 4 + y) * 2 + x) * 4 + kk, (((y * 2 + chunk) * 4 + z) * 2 + x) * 4 + kk

    def prev(key):
        same = (key[:, None] == key[None, :]) & (t[:, None] < t[None, :])
        found = jnp.max(jnp.where(same, t[:, None], -1), axis=0)
        return jnp.where(found < 0, NT, found)

    def last(key, count):
        ids = jnp.arange(count, dtype=jnp.int32)
        found = jnp.max(jnp.where(key[:, None] == ids[None, :], t[:, None], -1), axis=0)
        return jnp.where(found < 0, NT, found)

    c0, c1 = order(col)
    drow = (row // 8) * 10 + row % 8
    return jnp.concatenate(
        [drow, c0, c1, prev(col), prev(row), last(c0, CT), last(c1, CT), last(row, RT)]
    )


def split(v):
    hi = v.astype(BF16).astype(F32)
    return hi, v - hi


class Copies:
    def __init__(self, make):
        self.make = make

    def __getitem__(self, i):
        return self.make(i)


def kernel(
    tab, w0, dem_in, lead_in, a_hbm, cost_in, prim_in, dual_in,
    prim_out, dual_out, w_out,
    dem, lead, cost, prim0, dual0,
    af, wt, s0, s1, xg0, xg1, pb, fb, rb, qb, tb, dg0, dg1, yb, cr, pr, rhs, lag, wgt, fs, fa, fp,
    in_sem, a_sem, lag_s, lag_r, ca_s, ca_r, rz_s, rz_r, rp_s, rp_r, ap_s, ap_r, az_s, az_r, cs_s, cs_r,
    fi_s, fi_r,
):
    b = lax.axis_index("band")
    q = lax.axis_index("col")
    y, x, z = b // 8, (b // 4) % 2, b % 4
    xg, dg, s_buf = (xg0, xg1), (dg0, dg1), (s0, s1)
    both = range(2)

    def rc(src, dst, ss, rs, band, col):
        return pltpu.make_async_remote_copy(
            src_ref=src, dst_ref=dst, send_sem=ss, recv_sem=rs,
            device_id=(band, col), device_id_type=MESH,
        )

    g_of = (z, y)
    m_of = (y * 2 + x, z * 2 + x)

    def band_of(h, g, m):
        o, xx = m // 2, m % 2
        return o * 8 + xx * 4 + g if h == 0 else g * 8 + xx * 4 + o

    near = [
        (band_of(0, (z + i) % 4, m_of[0]), (q + j) % 4) for i in range(4) for j in range(4) if i or j
    ]
    plane = [(band_of(0, z, (m_of[0] + j) % 8), q) for j in range(1, 8)]

    def a_copy(i):
        n = NT // CHUNKS
        return pltpu.make_async_copy(a_hbm.at[pl.ds(i * n, n)], af.at[pl.ds(i * n, n)], a_sem.at[i])

    def lag_copy(l):
        return rc(dem, lag.at[l - 1], lag_s.at[l - 1], lag_r.at[l - 1], (b + l) % 32, q)

    def ca_copy(h, j):
        own = dg[h].at[pl.ds(q * 10, 10)]
        return rc(own, own, ca_s.at[h, j - 1], ca_r.at[h, j - 1], b, (q + j) % 4)

    def ca_recv(h, j):
        slot = dg[h].at[pl.ds(((q + 4 - j) % 4) * 10, 10)]
        return rc(slot, slot, ca_s.at[h, j - 1], ca_r.at[h, j - 1], b, (q + 4 - j) % 4)

    def ring(h):
        g = g_of[h]
        return g, (g + 1) % 4, (g + 3) % 4, (g + 2) % 4

    def half_of(c, half):
        return ((0, 18), (18, 16))[half] if c == 0 else ((34, 16), (50, 16))[half]

    def rz_copies(h, c):
        g, up, dn, opp = ring(h)
        m = m_of[h]
        bu, bd = band_of(h, up, m), band_of(h, dn, m)

        def piece(block, half):
            at, n = half_of(c, half)
            return pb.at[h, pl.ds(block * 66 + at, n)]

        def into(side, half):
            at, n = half_of(c, half)
            return rb.at[h, side, pl.ds(at, n)]

        def make(i):
            src, dst, to = (
                lambda: (piece(opp, 0), fb.at[h, c, 0, pl.ds(0, half_of(c, 0)[1])], bu),
                lambda: (piece(opp, 1), fb.at[h, c, 1, pl.ds(0, 16)], bd),
                lambda: (piece(up, 1), into(0, 1), bu),
                lambda: (piece(dn, 0), into(1, 0), bd),
                lambda: (piece(up, 0), into(0, 0), bu),
                lambda: (piece(dn, 1), into(1, 1), bd),
            )[i]()
            return rc(src, dst, rz_s.at[h, c, i], rz_r.at[h, c, i], to, q)

        return Copies(make)

    def rp_copy(h, c, j):
        m2 = (m_of[h] + j) % 8
        n = pl.ds(0, 4 if c else 6)
        return rc(
            qb.at[h, c, m2, n], tb.at[h, c, j - 1, n], rp_s.at[h, c, j - 1], rp_r.at[h, c, j - 1],
            band_of(h, g_of[h], m2), q,
        )

    def ap_copy(h, c, j, back=False):
        m = m_of[h]
        m2 = (m + 8 - j) % 8 if back else (m + j) % 8
        slot = xg[h].at[pl.ds(((g_of[h] * 2 + c) * 8 + (m2 if back else m)) * 4, 4)]
        return rc(slot, slot, ap_s.at[h, c, j - 1], ap_r.at[h, c, j - 1], band_of(h, g_of[h], m2), q)

    def az_copies(h, c, back=False):
        g, up, dn, opp = ring(h)
        m = m_of[h]
        bu, bd = band_of(h, up, m), band_of(h, dn, m)
        lo, hi = (dn, up) if back else (g, g)
        spec = (
            (lo, 0, bu), (hi, 1, bd), (lo, 1, bu), (hi, 0, bd),
            (opp if back else dn, 0, bu), (opp if back else up, 1, bd),
        )

        def make(i):
            block, half, to = spec[i]
            slot = xg[h].at[pl.ds((block * 2 + c) * 32 + half * 16, 16)]
            return rc(slot, slot, az_s.at[h, c, i], az_r.at[h, c, i], to, q)

        return Copies(make)

    def cs_copy(h, j):
        q2 = (q + j) % 4
        return rc(yb.at[h, pl.ds(q2 * 8, 8)], cr.at[h, j - 1], cs_s.at[h, j - 1], cs_r.at[h, j - 1], b, q2)

    inputs = [
        pltpu.make_async_copy(src, dst, in_sem.at[i])
        for i, (src, dst) in enumerate(
            ((dual_in, dual0), (dem_in, dem), (prim_in, prim0), (cost_in, cost), (lead_in, lead))
        )
    ]
    for c in inputs:
        c.start()
    for i in range(CHUNKS):
        a_copy(i).start()
    greeted = near + plane
    greeted = greeted + [(band_of(1, y, (m_of[1] + j) % 8), q) for j in range(1, 8)]
    greeted = greeted + [(band_of(1, (y + j) % 4, m_of[1]), q) for j in (1, 3)]
    greeted = greeted + [((b + l) % 32, q) for l in (1, 2, 3, 4, 28, 29, 30, 31)]
    barrier = pltpu.get_barrier_semaphore()
    for to in greeted:
        pl.semaphore_signal(barrier, inc=1, device_id=to, device_id_type=MESH)
    zero = jnp.zeros((8, T), F32)
    sublane = lax.broadcasted_iota(jnp.int32, (8, T), 0)
    lane = lax.broadcasted_iota(jnp.int32, (8, T), 1)
    for c in inputs:
        c.wait()
    for h in both:
        for k in range(8):
            dg[h][q * 10 + k] = dual0[8 * h:8 * h + 8, k * T:(k + 1) * T]
            pr[h, k] = prim0[8 * h:8 * h + 8, k * T:(k + 1) * T]
        dg[h][q * 10 + 8] = zero
        dg[h][q * 10 + 9] = zero
        weight = zero
        for i in range(8):
            weight = jnp.where(sublane == i, w0[8 * h + i], weight)
        wgt[h] = weight
        s_buf[h][NT] = zero
    pl.semaphore_wait(barrier, len(greeted))
    for h in both:
        for j in (2, 1, 3):
            ca_copy(h, j).start()
    for l in range(1, LEAD_MAX + 1):
        lag_copy(l).start()

    for i in range(CHUNKS):
        a_copy(i).wait()
        n = NT // CHUNKS

        def prep(t, carry):
            v = af[t]
            hi = v.astype(BF16)
            wt[t, 0] = hi
            wt[t, 1] = (v - hi.astype(F32)).astype(BF16)
            return carry

        lax.fori_loop(i * n, (i + 1) * n, prep, 0, unroll=2)

    def products(src, offsets, o_prev, forward):
        def pair(p, carry):
            ts = (2 * p, 2 * p + 1)
            rows = []
            for t in ts:
                for h in both:
                    rows += split(src[h][tab[offsets[h] + t]])
            lhs = jnp.concatenate(rows, axis=0).astype(BF16)
            lhs = jnp.concatenate([lhs, lhs], axis=1)
            (h1, l1), (h2, l2) = [(wt[t, 0], wt[t, 1]) for t in ts]
            if forward:
                quarters, contract = (h1, l1, h2, l2), 1
            else:
                quarters, contract = (h1, h2, l1, l2), 0
            w = jnp.concatenate(
                [jnp.concatenate(quarters[:2], axis=1), jnp.concatenate(quarters[2:], axis=1)], axis=0
            )
            out = lax.dot_general(lhs, w, (((1,), (contract,)), ((), ())), preferred_element_type=F32)
            for i, t in enumerate(ts):
                before = tab[o_prev + t]
                for h in both:
                    at, lanes = 32 * i + 16 * h, slice(i * T, (i + 1) * T)
                    s_buf[h][t] = out[at:at + 8, lanes] + out[at + 8:at + 16, lanes] + s_buf[h][before]
            return carry

        lax.fori_loop(0, NT // 2, pair, 0, unroll=8)

    def place(which, c, stat):
        blocks = [ring(h)[which] for h in both]
        if c == 0:
            for h in both:
                for e in range(2):
                    pb[h, blocks[h] * 66 + e] = stat[h][e]

        def one(i, carry):
            for h in both:
                last = tab[(O_L0, O_L1)[h] + blocks[h] * 64 + c * 32 + i]
                pb[h, blocks[h] * 66 + (34 if c else 2) + i] = s_buf[h][last]
            return carry

        lax.fori_loop(0, 32, one, 0, unroll=8)

    def start_ring(which, c, stat, copies):
        place(which, c, stat)
        for i in copies:
            for h in both:
                rz_copies(h, c)[i].start()

    def relay_ring(c):
        for h in both:
            g, up, dn, opp = ring(h)
            copies = rz_copies(h, c)
            at, n = half_of(c, 0)
            copies[0].wait_recv()
            here = pl.ds(up * 66 + at, n)
            pb[h, here] = pb[h, here] + fb[h, c, 0, 0:n]
            copies[4].start()
            at, n = half_of(c, 1)
            copies[1].wait_recv()
            here = pl.ds(dn * 66 + at, n)
            pb[h, here] = pb[h, here] + fb[h, c, 1, 0:n]
            copies[5].start()

    def start_plane(c):
        for h in both:
            copies = rz_copies(h, c)
            for i in (2, 3, 4, 5):
                copies[i].wait_recv()

            def ring_sum(i):
                return pb[h, g_of[h] * 66 + i] + rb[h, 0, i] + rb[h, 1, i]

            for m in range(8):
                for k in range(4):
                    qb[h, c, m, k] = ring_sum((34 if c else 2) + m * 4 + k)
            if c == 0:
                for e in range(2):
                    stat = ring_sum(e)
                    for m in range(8):
                        qb[h, c, m, 4 + e] = stat
            for j in (4, 3, 5, 2, 6, 1, 7):
                rp_copy(h, c, j).start()

    def new_weight(old, primal_square, dual_square):
        return jnp.sqrt(old * jnp.sqrt((primal_square + epsilon) / (dual_square + epsilon)))

    def update(c, it, squares):
        for h in both:
            m = m_of[h]
            for j in range(1, 8):
                rp_copy(h, c, j).wait_recv()

            def total(k):
                return qb[h, c, m, k] + sum(tb[h, c, j, k] for j in range(7))

            if c == 0:
                psq = jnp.sum(total(4), axis=1, keepdims=True)
                dsq = jnp.sum(total(5), axis=1, keepdims=True)
                old = wgt[h]
                wgt[h] = jnp.where(it > 0, new_weight(old, psq, dsq), old)
            pstep = step_scale / wgt[h]
            for kk in range(4):
                k = c * 4 + kk
                primal = pr[h, k]
                new = jnp.maximum(primal - pstep * (cost[k:k + 1, :] - total(kk)), 0.0)
                change = new - primal
                squares[h] = squares[h] + change * change
                pr[h, k] = new
                xg[h][((g_of[h] * 2 + c) * 8 + m) * 4 + kk] = 2.0 * new - primal
            for j in (4, 3, 5, 2, 6, 1, 7):
                ap_copy(h, c, j).start()

    def start_spread(c):
        for h in both:
            for j in range(1, 8):
                ap_copy(h, c, j, True).wait_recv()
            copies = az_copies(h, c)
            for i in range(4):
                copies[i].start()

    def relay_spread(c):
        for h in both:
            back, copies = az_copies(h, c, True), az_copies(h, c)
            back[0].wait_recv()
            copies[4].start()
            back[1].wait_recv()
            copies[5].start()

    def iteration(it, carry):
        for h in both:
            for j in range(1, 4):
                ca_recv(h, j).wait_recv()
        products(dg, (O_ROW, O_ROW), O_PC, False)
        stat = [[sum(dg[h][c * 10 + 8 + e] for c in range(4)) for e in range(2)] for h in both]
        start_ring(3, 0, stat, (0, 1))
        start_ring(1, 0, stat, (2,))
        start_ring(2, 0, stat, (3,))
        start_ring(0, 0, stat, ())
        place(3, 1, stat)
        relay_ring(0)
        for i in (0, 1):
            for h in both:
                rz_copies(h, 1)[i].start()
        start_ring(1, 1, stat, (2,))
        start_ring(2, 1, stat, (3,))
        start_ring(0, 1, stat, ())
        start_plane(0)
        relay_ring(1)
        start_plane(1)
        squares = [zero, zero]
        update(0, it, squares)
        update(1, it, squares)
        for h in both:
            for j in range(1, 4):
                ca_copy(h, j).wait_send()
            dg[h][q * 10 + 8] = squares[h]
        start_spread(0)
        relay_spread(0)
        start_spread(1)
        relay_spread(1)

        @pl.when(it == 0)
        def _():
            for l in range(1, LEAD_MAX + 1):
                lag_copy(l).wait_recv()
            for h in both:
                rows = slice(8 * h, 8 * h + 8)
                for k in range(8):
                    lanes = slice(k * T, (k + 1) * T)
                    periods = jnp.broadcast_to(lead[k:k + 1, :], (8, T))
                    lagged = jnp.zeros((8, T), F32)
                    for l in range(1, LEAD_MAX + 1):
                        lagged = jnp.where(periods == l, lag[l - 1, rows, lanes], lagged)
                    rhs[h, k] = dem[rows, lanes] - return_share * lagged
            for l in range(1, LEAD_MAX + 1):
                lag_copy(l).wait_send()

        for c in range(2):
            for h in both:
                back = az_copies(h, c, True)
                for i in (2, 3, 4, 5):
                    back[i].wait_recv()
        products(xg, (O_C0, O_C1), O_PR, True)
        for h in both:
            for r in range(RT):
                yb[h, r] = s_buf[h][tab[O_LR + r]]
            for j in (2, 1, 3):
                cs_copy(h, j).start()
        for h in both:
            for j in range(1, 4):
                cs_copy(h, j).wait_recv()
            dstep = step_scale * wgt[h]
            square = zero
            for k in range(8):
                push = yb[h, q * 8 + k] + (cr[h, 0, k] + cr[h, 1, k] + cr[h, 2, k])
                old = dg[h][q * 10 + k]
                new = old + dstep * (rhs[h, k] - push)
                change = new - old
                square = square + change * change
                dg[h][q * 10 + k] = new
            dg[h][q * 10 + 9] = square

            @pl.when(it < ITERS - 1)
            def _():
                for j in (2, 1, 3):
                    ca_copy(h, j).start()

        for h in both:
            for c in range(2):
                for copies in (rz_copies(h, c), az_copies(h, c)):
                    for i in range(6):
                        copies[i].wait_send()
                for j in range(1, 8):
                    rp_copy(h, c, j).wait_send()
                    ap_copy(h, c, j).wait_send()
            for j in range(1, 4):
                cs_copy(h, j).wait_send()
        return carry

    lax.fori_loop(0, ITERS, iteration, 0)

    packed = zero
    for h in both:
        for e in range(2):
            packed = jnp.where(
                lane == 2 * h + e, jnp.sum(dg[h][q * 10 + 8 + e], axis=1, keepdims=True), packed
            )
    fs[0] = packed
    for stage, (group, dst, at) in enumerate(((near, fa, 0), (plane, fp, 15))):
        copies = [
            rc(fs.at[stage], dst.at[i], fi_s.at[at + i], fi_r.at[at + i], *to) for i, to in enumerate(group)
        ]
        for c in copies:
            c.start()
        if stage == 0:
            for h in both:
                for k in range(8):
                    prim_out[8 * h:8 * h + 8, k * T:(k + 1) * T] = pr[h, k]
                    dual_out[8 * h:8 * h + 8, k * T:(k + 1) * T] = dg[h][q * 10 + k]
        for c in copies:
            c.wait_recv()
        fs[stage + 1] = fs[stage] + sum(dst[i] for i in range(len(copies)))
        for c in copies:
            c.wait_send()
    sums = fs[2]
    for h in both:
        psq, dsq = [
            jnp.sum(jnp.where(lane == 2 * h + e, sums, 0.0), axis=1, keepdims=True) for e in range(2)
        ]
        w_out[8 * h:8 * h + 8, :] = new_weight(wgt[h], psq, dsq)


def on_device(
    demand, lead_periods, matrix_tiles, tile_pos, cost_vector, primal_init, dual_init, weight_init
):
    table = index_table(tile_pos)
    vmem = pl.BlockSpec(memory_space=pltpu.VMEM)
    smem = pl.BlockSpec(memory_space=pltpu.SMEM)
    hbm = pl.BlockSpec(memory_space=pl.ANY)
    dma = pltpu.SemaphoreType.DMA

    def buf(*shape, dtype=F32):
        return pltpu.VMEM(shape, dtype)

    primal, dual, weight = pl.pallas_call(
        kernel,
        out_shape=(
            jax.ShapeDtypeStruct((16, 1024), F32),
            jax.ShapeDtypeStruct((16, 1024), F32),
            jax.ShapeDtypeStruct((16, T), F32),
        ),
        in_specs=[smem, smem] + [hbm] * 6,
        out_specs=(vmem, vmem, vmem),
        scratch_shapes=[
            buf(16, 1024),
            buf(8, T, dtype=jnp.int32),
            buf(8, T),
            buf(16, 1024),
            buf(16, 1024),
            buf(NT, T, T),
            buf(NT, 2, T, T, dtype=BF16),
            buf(NT + 1, 8, T),
            buf(NT + 1, 8, T),
            buf(CT, 8, T),
            buf(CT, 8, T),
            buf(2, 264, 8, T),
            buf(2, 2, 2, 18, 8, T),
            buf(2, 2, 66, 8, T),
            buf(2, 2, 8, 6, 8, T),
            buf(2, 2, 7, 6, 8, T),
            buf(40, 8, T),
            buf(40, 8, T),
            buf(2, RT, 8, T),
            buf(2, 3, 8, 8, T),
            buf(2, 8, 8, T),
            buf(2, 8, 8, T),
            buf(4, 16, 1024),
            buf(2, 8, T),
            buf(3, 8, T),
            buf(15, 8, T),
            buf(7, 8, T),
            dma((5,)), dma((CHUNKS,)), dma((4,)), dma((4,)),
            dma((2, 3)), dma((2, 3)), dma((2, 2, 6)), dma((2, 2, 6)), dma((2, 2, 7)), dma((2, 2, 7)),
            dma((2, 2, 7)), dma((2, 2, 7)), dma((2, 2, 6)), dma((2, 2, 6)), dma((2, 3)), dma((2, 3)),
            dma((22,)), dma((22,)),
        ],
        compiler_params=pltpu.CompilerParams(
            collective_id=0, has_side_effects=True, vmem_limit_bytes=60 * 2**20
        ),
    )(
        table,
        weight_init,
        demand.T,
        lead_periods.reshape(8, T),
        matrix_tiles.reshape(NT, T, T),
        cost_vector.reshape(8, T),
        primal_init.T,
        dual_init.T,
    )
    return primal.T, dual.T, weight[:, 0]


def solution(mesh):
    in_specs = (
        P(("band", "col"), None),
        P(("band", "col")),
        P("band", "col", None, None, None),
        P("band", "col", None),
        P(("band", "col")),
        P(("band", "col"), None),
        P(("band", "col"), None),
        P(),
    )
    out_specs = (P(("band", "col"), None), P(("band", "col"), None), P())
    return jax.shard_map(
        on_device, mesh=mesh, in_specs=in_specs, out_specs=out_specs, check_vma=False
    )
```

```python
import jax
import jax.numpy as jnp
from jax import lax
from jax.experimental import pallas as pl
from jax.experimental.pallas import tpu as pltpu
from jax.sharding import PartitionSpec as P

ITERS = 3
LEAD_MAX = 4
step_scale = 0.45
return_share = 0.6
epsilon = 1e-06

NT = 128
T = 128
CT = 256
RT = 32
F32 = jnp.float32
BF16 = jnp.bfloat16
CHUNKS = 16
MESH = pl.DeviceIdType.MESH

O_ROW, O_C, O_PC, O_PR, O_LC, O_LR = 0, 128, 256, 384, 512, 768


def index_table(pos):
    pos = pos.reshape(-1)
    t = jnp.arange(NT, dtype=jnp.int32)
    row, col = pos // CT, pos % CT

    def order(c):
        k, z, x, y = c % 8, (c // 8) % 4, (c // 32) % 2, c // 64
        kk = k % 4
        return jnp.where(k < 4, ((z * 4 + y) * 2 + x) * 4 + kk, 128 + ((y * 4 + z) * 2 + x) * 4 + kk)

    def prev(key):
        same = (key[:, None] == key[None, :]) & (t[:, None] < t[None, :])
        found = jnp.max(jnp.where(same, t[:, None], -1), axis=0)
        return jnp.where(found < 0, NT, found)

    def last(key, count):
        ids = jnp.arange(count, dtype=jnp.int32)
        found = jnp.max(jnp.where(key[:, None] == ids[None, :], t[:, None], -1), axis=0)
        return jnp.where(found < 0, NT, found)

    drow = (row // 8) % 2 * 17 + row // 16 * 8 + row % 8
    return jnp.concatenate(
        [drow, order(col), prev(col), prev(row), last(order(col), CT), last(row, RT)]
    )


def split(v):
    hi = v.astype(BF16).astype(F32)
    return hi, v - hi


def kernel(
    tab, w0, dem_in, lead_in, a_hbm, cost_in, prim_in, dual_in,
    prim_out, dual_out, w_out,
    dem, lead, cost, prim0, dual0,
    af, wt, s0, s1, xg0, xg1, pb, rb, qb, tb, dg0, dg1, yb, yc, ych, yx, pr, rhs, lag, wgt, fs, fc, fa,
    in_sem, a_sem, lag_s, lag_r, ca_s, ca_r, rz_s, rz_r, rp_s, rp_r, ap_s, ap_r, az_s, az_r, col_s, col_r,
    sums_r, rh_s, rh_r, fi_s, fi_r,
):
    b = lax.axis_index("band")
    q = lax.axis_index("col")
    y, x, z = b // 8, (b // 4) % 2, b % 4
    xg, dg, s_buf = (xg0, xg1), (dg0, dg1), (s0, s1)
    both = range(2)

    def rc(src, dst, ss, rs, band, col):
        return pltpu.make_async_remote_copy(
            src_ref=src, dst_ref=dst, send_sem=ss, recv_sem=rs,
            device_id=(band, col), device_id_type=MESH,
        )

    g_of = (z, y)
    m_of = (y * 2 + x, z * 2 + x)

    def band_of(c, g, m):
        o, xx = m // 2, m % 2
        return o * 8 + xx * 4 + g if c == 0 else g * 8 + xx * 4 + o

    band = [((b + i) % 32, q) for i in range(1, 32)]
    core, chip = q % 2, q // 2
    other_core, other_chip = q + 1 - 2 * core, (q + 2) % 4

    def a_copy(i):
        n = NT // CHUNKS
        return pltpu.make_async_copy(a_hbm.at[pl.ds(i * n, n)], af.at[pl.ds(i * n, n)], a_sem.at[i])

    def lag_copy(l):
        return rc(dem, lag.at[l - 1], lag_s.at[l - 1], lag_r.at[l - 1], (b + l) % 32, q)

    def ca_copy(h, j):
        own = dg[h].at[pl.ds(core * 17 + chip * 8, 8)]
        return rc(own, own, ca_s.at[h, j - 1], ca_r.at[h, j - 1], b, (q + j) % 4)

    def ca_recv(h, j):
        q2 = (q + 4 - j) % 4
        slot = dg[h].at[pl.ds(q2 % 2 * 17 + q2 // 2 * 8, 8)]
        return rc(slot, slot, ca_s.at[h, j - 1], ca_r.at[h, j - 1], b, q2)

    def terms_copy(h):
        return rc(yb.at[h, 1 - core], yc.at[h], col_s.at[0, h], col_r.at[0, h], b, other_core)

    def sums_copy(h, it):
        return rc(ych.at[h], yx.at[h, it], col_s.at[1, h], sums_r.at[h, it], b, other_chip)

    def prices_copy(h, back=False):
        slot = dg[h].at[pl.ds((1 - core if back else core) * 17, 17)]
        return rc(slot, slot, col_s.at[2, h], col_r.at[2, h], b, other_core)

    def rhs_copy(h, back=False):
        slot = rhs.at[h, pl.ds((1 - chip if back else chip) * 8, 8)]
        return rc(slot, slot, rh_s.at[h], rh_r.at[h], b, other_chip)

    def rz_copy(h, c, j):
        g2 = (g_of[c] + j) % 4
        part = pl.ds(1, 32) if c else pl.ds(0, 33)
        return rc(
            pb.at[h, c, g2, part], rb.at[h, c, j - 1, part], rz_s.at[h, c, j - 1], rz_r.at[h, c, j - 1],
            band_of(c, g2, m_of[c]), q,
        )

    def rp_copy(h, c, j):
        m2 = (m_of[c] + j) % 8
        part = pl.ds(1, 4) if c else pl.ds(0, 5)
        return rc(
            qb.at[h, c, m2, part], tb.at[h, c, j - 1, part], rp_s.at[h, c, j - 1], rp_r.at[h, c, j - 1],
            band_of(c, g_of[c], m2), q,
        )

    def ap_copy(h, c, j, back=False):
        m = m_of[c]
        m2 = (m + 8 - j) % 8 if back else (m + j) % 8
        slot = xg[h].at[pl.ds(c * 128 + g_of[c] * 32 + (m2 if back else m) * 4, 4)]
        return rc(slot, slot, ap_s.at[h, c, j - 1], ap_r.at[h, c, j - 1], band_of(c, g_of[c], m2), q)

    def az_copy(h, c, j, back=False):
        g = g_of[c]
        g2 = (g + 4 - j) % 4 if back else (g + j) % 4
        slot = xg[h].at[pl.ds(c * 128 + (g2 if back else g) * 32, 32)]
        return rc(slot, slot, az_s.at[h, c, j - 1], az_r.at[h, c, j - 1], band_of(c, g2, m_of[c]), q)

    inputs = [
        pltpu.make_async_copy(src, dst, in_sem.at[i])
        for i, (src, dst) in enumerate(
            ((dual_in, dual0), (dem_in, dem), (prim_in, prim0), (cost_in, cost), (lead_in, lead))
        )
    ]
    for c in inputs:
        c.start()
    for i in range(CHUNKS):
        a_copy(i).start()
    greeted = band + [(b, (q + j) % 4) for j in (1, 2, 3)]
    barrier = pltpu.get_barrier_semaphore()
    for to in greeted:
        pl.semaphore_signal(barrier, inc=1, device_id=to, device_id_type=MESH)
    zero = jnp.zeros((8, T), F32)
    sublane = lax.broadcasted_iota(jnp.int32, (8, T), 0)
    lane = lax.broadcasted_iota(jnp.int32, (8, T), 1)
    for c in inputs:
        c.wait()
    for h in both:
        for k in range(8):
            dg[h][core * 17 + chip * 8 + k] = dual0[8 * h:8 * h + 8, k * T:(k + 1) * T]
            pr[h, k] = prim0[8 * h:8 * h + 8, k * T:(k + 1) * T]
        dg[h][16] = zero
        dg[h][33] = zero
        weight = zero
        for i in range(8):
            weight = jnp.where(sublane == i, w0[8 * h + i], weight)
        wgt[h] = weight
        s_buf[h][NT] = zero

    def prep_chunks(first, end):
        n = NT // CHUNKS

        def prep(t, carry):
            v = af[t]
            hi = v.astype(BF16)
            wt[t, 0] = hi
            wt[t, 1] = (v - hi.astype(F32)).astype(BF16)
            return carry

        for i in range(first, end):
            a_copy(i).wait()
            lax.fori_loop(i * n, (i + 1) * n, prep, 0, unroll=2)

    prep_chunks(0, CHUNKS // 2)
    pl.semaphore_wait(barrier, len(greeted))
    for h in both:
        for j in (2, 1, 3):
            ca_copy(h, j).start()
    for l in range(1, LEAD_MAX + 1):
        lag_copy(l).start()
    prep_chunks(CHUNKS // 2, CHUNKS)

    def products(h, src, o_src, o_prev, forward):
        def pair(p, carry):
            ts = (2 * p, 2 * p + 1)
            rows = []
            for t in ts:
                rows += split(src[tab[o_src + t]])
            lhs = jnp.concatenate(rows, axis=0).astype(BF16)
            lhs = jnp.concatenate([lhs, lhs], axis=1)
            (h1, l1), (h2, l2) = [(wt[t, 0], wt[t, 1]) for t in ts]
            if forward:
                quarters, contract = (h1, l1, h2, l2), 1
            else:
                quarters, contract = (h1, h2, l1, l2), 0
            w = jnp.concatenate(
                [jnp.concatenate(quarters[:2], axis=1), jnp.concatenate(quarters[2:], axis=1)], axis=0
            )
            out = lax.dot_general(lhs, w, (((1,), (contract,)), ((), ())), preferred_element_type=F32)
            for i, t in enumerate(ts):
                at, lanes = 16 * i, slice(i * T, (i + 1) * T)
                s_buf[h][t] = out[at:at + 8, lanes] + out[at + 8:at + 16, lanes] + s_buf[h][tab[o_prev + t]]
            return carry

        lax.fori_loop(0, NT // 2, pair, 0, unroll=16)

    def place(h, c, g, stat):
        if c == 0:
            pb[h, c, g, 0] = stat

        def one(i, carry):
            pb[h, c, g, 1 + i] = s_buf[h][tab[O_LC + c * 128 + g * 32 + i]]
            return carry

        lax.fori_loop(0, 32, one, 0, unroll=16)

    def start_ring(h, stat):
        for j in (2, 1, 3, 0):
            for c in range(2):
                place(h, c, (g_of[c] + j) % 4, stat)
                if j:
                    rz_copy(h, c, j).start()

    def start_plane(h):
        for c in range(2):
            for j in (1, 3, 2):
                rz_copy(h, c, j).wait_recv()

            def ring_sum(i):
                return (pb[h, c, g_of[c], i] + rb[h, c, 0, i]) + (rb[h, c, 1, i] + rb[h, c, 2, i])

            for m in range(8):
                for k in range(4):
                    qb[h, c, m, 1 + k] = ring_sum(1 + m * 4 + k)
            if c == 0:
                stat = ring_sum(0)
                for m in range(8):
                    qb[h, c, m, 0] = stat
            for j in (4, 3, 5, 2, 6, 1, 7):
                rp_copy(h, c, j).start()

    def new_weight(old, sums, at):
        psq, dsq = [
            jnp.sum(jnp.where(lane == at + e, sums, 0.0), axis=1, keepdims=True) for e in range(2)
        ]
        return jnp.sqrt(old * jnp.sqrt((psq + epsilon) / (dsq + epsilon)))

    def lanes_sum(v):
        return jnp.sum(v, axis=1, keepdims=True)

    def update(h, it):
        square = zero
        for c in range(2):
            m = m_of[c]
            for j in range(1, 8):
                rp_copy(h, c, j).wait_recv()

            def total(k):
                return qb[h, c, m, k] + sum(tb[h, c, j, k] for j in range(7))

            if c == 0:
                old = wgt[h]
                wgt[h] = jnp.where(it > 0, new_weight(old, total(0), 0), old)
            pstep = step_scale / wgt[h]
            for kk in range(4):
                k = c * 4 + kk
                primal = pr[h, k]
                new = jnp.maximum(primal - pstep * (cost[k:k + 1, :] - total(1 + kk)), 0.0)
                change = new - primal
                square = square + change * change
                pr[h, k] = new
                xg[h][c * 128 + g_of[c] * 32 + m * 4 + kk] = 2.0 * new - primal
            for j in (4, 3, 5, 2, 6, 1, 7):
                ap_copy(h, c, j).start()
        yb[h, 1 - core, 16] = square
        yb[h, core, 16] = square

    def start_spread(h):
        for c in range(2):
            for j in range(1, 8):
                ap_copy(h, c, j, True).wait_recv()
            for j in (2, 1, 3):
                az_copy(h, c, j).start()

    def iteration(it, carry):
        for h in both:
            @pl.when(it == 0)
            def _():
                for j in range(1, 4):
                    ca_recv(h, j).wait_recv()

            @pl.when(it > 0)
            def _():
                prices_copy(h, True).wait_recv()

            products(h, dg[h], O_ROW, O_PC, False)
            start_ring(h, jnp.where(lane == 0, dg[h][16], dg[h][16] + dg[h][33]))
        for h in both:
            start_plane(h)
        for h in both:
            update(h, it)
        for h in both:
            start_spread(h)

        @pl.when(it == 0)
        def _():
            for l in range(1, LEAD_MAX + 1):
                lag_copy(l).wait_recv()
            for h in both:
                rows = slice(8 * h, 8 * h + 8)
                for k in range(8):
                    lanes = slice(k * T, (k + 1) * T)
                    periods = jnp.broadcast_to(lead[k:k + 1, :], (8, T))
                    lagged = jnp.zeros((8, T), F32)
                    for l in range(1, LEAD_MAX + 1):
                        lagged = jnp.where(periods == l, lag[l - 1, rows, lanes], lagged)
                    rhs[h, chip * 8 + k] = dem[rows, lanes] - return_share * lagged
                rhs_copy(h).start()
            for l in range(1, LEAD_MAX + 1):
                lag_copy(l).wait_send()

        for h in both:
            for c in range(2):
                for j in (1, 3, 2):
                    az_copy(h, c, j, True).wait_recv()
            products(h, xg[h], O_C, O_PR, True)
            for r in range(RT):
                yb[h, r // 8 % 2, r // 16 * 8 + r % 8] = s_buf[h][tab[O_LR + r]]
            terms_copy(h).start()
        for h in both:
            terms_copy(h).wait_recv()
            ych[h] = yb[h, core] + yc[h]
            sums_copy(h, it).start()
        for h in both:
            @pl.when(it == 0)
            def _():
                rhs_copy(h, True).wait_recv()
                rhs_copy(h).wait_send()
                for j in range(1, 4):
                    ca_copy(h, j).wait_send()

            @pl.when(it > 0)
            def _():
                prices_copy(h).wait_send()

            sums_copy(h, it).wait_recv()
            dstep = step_scale * wgt[h]
            square = zero
            for k in range(16):
                push = ych[h, k] + yx[h, it, k]
                old = dg[h][core * 17 + k]
                new = old + dstep * (rhs[h, k] - push)
                change = new - old
                square = square + change * change
                dg[h][core * 17 + k] = new
            primal_square = lanes_sum(ych[h, 16] + yx[h, it, 16])
            dg[h][core * 17 + 16] = jnp.where(
                lane == 0, primal_square, jnp.where(lane == 1, lanes_sum(square), 0.0)
            )

            @pl.when(it < ITERS - 1)
            def _():
                prices_copy(h).start()

        for h in both:
            for c in range(2):
                for j in range(1, 4):
                    rz_copy(h, c, j).wait_send()
                    az_copy(h, c, j).wait_send()
                for j in range(1, 8):
                    rp_copy(h, c, j).wait_send()
                    ap_copy(h, c, j).wait_send()
            terms_copy(h).wait_send()
            sums_copy(h, it).wait_send()
        return carry

    lax.fori_loop(0, ITERS, iteration, 0)

    packed = zero
    for h in both:
        stat = dg[h][core * 17 + 16]
        for e in range(2):
            value = lanes_sum(jnp.where(lane == e, stat, 0.0))
            packed = jnp.where(lane == 2 * h + e, value, packed)
    fs[0] = packed
    first = rc(fs.at[0], fc, fi_s.at[31], fi_r.at[31], b, other_core)
    first.start()
    for h in both:
        for k in range(8):
            prim_out[8 * h:8 * h + 8, k * T:(k + 1) * T] = pr[h, k]
            dual_out[8 * h:8 * h + 8, k * T:(k + 1) * T] = dg[h][core * 17 + chip * 8 + k]
    first.wait_recv()
    fs[1] = jnp.where(lane % 2 == 0, packed, packed + fc[...])
    copies = [rc(fs.at[1], fa.at[i], fi_s.at[i], fi_r.at[i], *to) for i, to in enumerate(band)]
    for c in copies:
        c.start()
    for c in copies:
        c.wait_recv()
    sums = fs[1] + jnp.sum(fa[...], axis=0)
    for h in both:
        w_out[8 * h:8 * h + 8, :] = new_weight(wgt[h], sums, 2 * h)
    first.wait_send()
    for c in copies:
        c.wait_send()


def on_device(
    demand, lead_periods, matrix_tiles, tile_pos, cost_vector, primal_init, dual_init, weight_init
):
    table = index_table(tile_pos)
    vmem = pl.BlockSpec(memory_space=pltpu.VMEM)
    smem = pl.BlockSpec(memory_space=pltpu.SMEM)
    hbm = pl.BlockSpec(memory_space=pl.ANY)
    dma = pltpu.SemaphoreType.DMA

    def buf(*shape, dtype=F32):
        return pltpu.VMEM(shape, dtype)

    primal, dual, weight = pl.pallas_call(
        kernel,
        out_shape=(
            jax.ShapeDtypeStruct((16, 1024), F32),
            jax.ShapeDtypeStruct((16, 1024), F32),
            jax.ShapeDtypeStruct((16, T), F32),
        ),
        in_specs=[smem, smem] + [hbm] * 6,
        out_specs=(vmem, vmem, vmem),
        scratch_shapes=[
            buf(16, 1024),
            buf(8, T, dtype=jnp.int32),
            buf(8, T),
            buf(16, 1024),
            buf(16, 1024),
            buf(NT, T, T),
            buf(NT, 2, T, T, dtype=BF16),
            buf(NT + 1, 8, T),
            buf(NT + 1, 8, T),
            buf(CT, 8, T),
            buf(CT, 8, T),
            buf(2, 2, 4, 33, 8, T),
            buf(2, 2, 3, 33, 8, T),
            buf(2, 2, 8, 5, 8, T),
            buf(2, 2, 7, 5, 8, T),
            buf(34, 8, T),
            buf(34, 8, T),
            buf(2, 2, 17, 8, T),
            buf(2, 17, 8, T),
            buf(2, 17, 8, T),
            buf(2, ITERS, 17, 8, T),
            buf(2, 8, 8, T),
            buf(2, 16, 8, T),
            buf(4, 16, 1024),
            buf(2, 8, T),
            buf(2, 8, T),
            buf(8, T),
            buf(31, 8, T),
            dma((5,)), dma((CHUNKS,)), dma((4,)), dma((4,)),
            dma((2, 3)), dma((2, 3)), dma((2, 2, 3)), dma((2, 2, 3)), dma((2, 2, 7)), dma((2, 2, 7)),
            dma((2, 2, 7)), dma((2, 2, 7)), dma((2, 2, 3)), dma((2, 2, 3)), dma((3, 2)), dma((3, 2)),
            dma((2, ITERS)), dma((2,)), dma((2,)), dma((32,)), dma((32,)),
        ],
        compiler_params=pltpu.CompilerParams(
            collective_id=0, has_side_effects=True, vmem_limit_bytes=60 * 2**20
        ),
    )(
        table,
        weight_init,
        demand.T,
        lead_periods.reshape(8, T),
        matrix_tiles.reshape(NT, T, T),
        cost_vector.reshape(8, T),
        primal_init.T,
        dual_init.T,
    )
    return primal.T, dual.T, weight[:, 0]


def solution(mesh):
    in_specs = (
        P(("band", "col"), None),
        P(("band", "col")),
        P("band", "col", None, None, None),
        P("band", "col", None),
        P(("band", "col")),
        P(("band", "col"), None),
        P(("band", "col"), None),
        P(),
    )
    out_specs = (P(("band", "col"), None), P(("band", "col"), None), P())
    return jax.shard_map(
        on_device, mesh=mesh, in_specs=in_specs, out_specs=out_specs, check_vma=False
    )
```

```python
import jax
import jax.numpy as jnp
from jax import lax
from jax.experimental import pallas as pl
from jax.experimental.pallas import tpu as pltpu
from jax.sharding import PartitionSpec as P

ITERS = 3
LEAD_MAX = 4
step_scale = 0.45
return_share = 0.6
epsilon = 1e-06

NT = 128
T = 128
CT = 256
RT = 32
F32 = jnp.float32
BF16 = jnp.bfloat16
CHUNKS = 16
MESH = pl.DeviceIdType.MESH

O_ROW, O_C, O_PC, O_PR, O_LC, O_LR = 0, 128, 256, 384, 512, 768


def index_table(pos):
    pos = pos.reshape(-1)
    t = jnp.arange(NT, dtype=jnp.int32)
    row, col = pos // CT, pos % CT

    def order(c):
        k, z, x, y = c % 8, (c // 8) % 4, (c // 32) % 2, c // 64
        kk = k % 4
        return jnp.where(k < 4, ((z * 4 + y) * 2 + x) * 4 + kk, 128 + ((y * 4 + z) * 2 + x) * 4 + kk)

    def prev(key):
        same = (key[:, None] == key[None, :]) & (t[:, None] < t[None, :])
        found = jnp.max(jnp.where(same, t[:, None], -1), axis=0)
        return jnp.where(found < 0, NT, found)

    def last(key, count):
        ids = jnp.arange(count, dtype=jnp.int32)
        found = jnp.max(jnp.where(key[:, None] == ids[None, :], t[:, None], -1), axis=0)
        return jnp.where(found < 0, NT, found)

    drow = (row // 8) % 2 * 17 + row // 16 * 8 + row % 8
    return jnp.concatenate(
        [drow, order(col), prev(col), prev(row), last(order(col), CT), last(row, RT)]
    )


def split(v):
    hi = v.astype(BF16).astype(F32)
    return hi, v - hi


def kernel(
    tab, w0, dem_in, lead_in, a_hbm, cost_in, prim_in, dual_in,
    prim_out, dual_out, w_out,
    dem, lead, cost, prim0, dual0,
    af, wt, s0, s1, xg0, xg1, pb, fb, rb, qb, tb, dg0, dg1, yb, yc, ych, yx, pr, rhs, lag, wgt, fs, fc, fa,
    in_sem, a_sem, lag_s, lag_r, ca_s, ca_r, rz_s, rz_r, rp_s, rp_r, ap_s, ap_r, az_s, az_r, col_s, col_r,
    sums_r, rh_s, rh_r, fi_s, fi_r,
):
    b = lax.axis_index("band")
    q = lax.axis_index("col")
    y, x, z = b // 8, (b // 4) % 2, b % 4
    xg, dg, s_buf = (xg0, xg1), (dg0, dg1), (s0, s1)
    both = range(2)

    def rc(src, dst, ss, rs, band, col):
        return pltpu.make_async_remote_copy(
            src_ref=src, dst_ref=dst, send_sem=ss, recv_sem=rs,
            device_id=(band, col), device_id_type=MESH,
        )

    g_of = (z, y)
    m_of = (y * 2 + x, z * 2 + x)

    def band_of(c, g, m):
        o, xx = m // 2, m % 2
        return o * 8 + xx * 4 + g if c == 0 else g * 8 + xx * 4 + o

    band = [((b + i) % 32, q) for i in range(1, 32)]
    core, chip = q % 2, q // 2
    other_core, other_chip = q + 1 - 2 * core, (q + 2) % 4

    def a_copy(i):
        n = NT // CHUNKS
        return pltpu.make_async_copy(a_hbm.at[pl.ds(i * n, n)], af.at[pl.ds(i * n, n)], a_sem.at[i])

    def lag_copy(l):
        return rc(dem, lag.at[l - 1], lag_s.at[l - 1], lag_r.at[l - 1], (b + l) % 32, q)

    def ca_copy(h, j):
        own = dg[h].at[pl.ds(core * 17 + chip * 8, 8)]
        return rc(own, own, ca_s.at[h, j - 1], ca_r.at[h, j - 1], b, (q + j) % 4)

    def ca_recv(h, j):
        q2 = (q + 4 - j) % 4
        slot = dg[h].at[pl.ds(q2 % 2 * 17 + q2 // 2 * 8, 8)]
        return rc(slot, slot, ca_s.at[h, j - 1], ca_r.at[h, j - 1], b, q2)

    def terms_copy(h):
        return rc(yb.at[h, 1 - core], yc.at[h], col_s.at[0, h], col_r.at[0, h], b, other_core)

    def sums_copy(h, it):
        return rc(ych.at[h], yx.at[h, it], col_s.at[1, h], sums_r.at[h, it], b, other_chip)

    def prices_copy(h, back=False):
        slot = dg[h].at[pl.ds((1 - core if back else core) * 17, 17)]
        return rc(slot, slot, col_s.at[2, h], col_r.at[2, h], b, other_core)

    def rhs_copy(h, back=False):
        slot = rhs.at[h, pl.ds((1 - chip if back else chip) * 8, 8)]
        return rc(slot, slot, rh_s.at[h], rh_r.at[h], b, other_chip)

    def ring(c):
        g = g_of[c]
        return g, (g + 1) % 4, (g + 3) % 4, (g + 2) % 4

    def half_of(c, half):
        return (17, 16) if half else (c, 17 - c)

    def rz_copy(h, c, i):
        g, up, dn, opp = ring(c)
        block, side, half = ((opp, 0, 0), (opp, 1, 1), (up, 0, 1), (dn, 1, 0), (up, 0, 0), (dn, 1, 1))[i]
        at, n = half_of(c, half)
        src = pb.at[h, c, block, pl.ds(at, n)]
        dst = fb.at[h, c, side, pl.ds(0, n)] if i < 2 else rb.at[h, c, side, pl.ds(at, n)]
        return rc(
            src, dst, rz_s.at[h, c, i], rz_r.at[h, c, i], band_of(c, dn if side else up, m_of[c]), q
        )

    def rp_copy(h, c, j):
        m2 = (m_of[c] + j) % 8
        part = pl.ds(1, 4) if c else pl.ds(0, 5)
        return rc(
            qb.at[h, c, m2, part], tb.at[h, c, j - 1, part], rp_s.at[h, c, j - 1], rp_r.at[h, c, j - 1],
            band_of(c, g_of[c], m2), q,
        )

    def ap_copy(h, c, j, back=False):
        m = m_of[c]
        m2 = (m + 8 - j) % 8 if back else (m + j) % 8
        slot = xg[h].at[pl.ds(c * 128 + g_of[c] * 32 + (m2 if back else m) * 4, 4)]
        return rc(slot, slot, ap_s.at[h, c, j - 1], ap_r.at[h, c, j - 1], band_of(c, g_of[c], m2), q)

    def az_copy(h, c, i, back=False):
        g, up, dn, opp = ring(c)
        lo, hi = (dn, up) if back else (g, g)
        block, half = (
            (lo, 0), (hi, 1), (lo, 1), (hi, 0), (opp if back else dn, 0), (opp if back else up, 1)
        )[i]
        slot = xg[h].at[pl.ds(c * 128 + block * 32 + half * 16, 16)]
        to = band_of(c, dn if i % 2 else up, m_of[c])
        return rc(slot, slot, az_s.at[h, c, i], az_r.at[h, c, i], to, q)

    inputs = [
        pltpu.make_async_copy(src, dst, in_sem.at[i])
        for i, (src, dst) in enumerate(
            ((dual_in, dual0), (dem_in, dem), (prim_in, prim0), (cost_in, cost), (lead_in, lead))
        )
    ]
    for c in inputs:
        c.start()
    for i in range(CHUNKS):
        a_copy(i).start()
    greeted = band + [(b, (q + j) % 4) for j in (1, 2, 3)]
    barrier = pltpu.get_barrier_semaphore()
    for to in greeted:
        pl.semaphore_signal(barrier, inc=1, device_id=to, device_id_type=MESH)
    zero = jnp.zeros((8, T), F32)
    sublane = lax.broadcasted_iota(jnp.int32, (8, T), 0)
    lane = lax.broadcasted_iota(jnp.int32, (8, T), 1)
    for c in inputs:
        c.wait()
    for h in both:
        for k in range(8):
            dg[h][core * 17 + chip * 8 + k] = dual0[8 * h:8 * h + 8, k * T:(k + 1) * T]
            pr[h, k] = prim0[8 * h:8 * h + 8, k * T:(k + 1) * T]
        dg[h][16] = zero
        dg[h][33] = zero
        weight = zero
        for i in range(8):
            weight = jnp.where(sublane == i, w0[8 * h + i], weight)
        wgt[h] = weight
        s_buf[h][NT] = zero

    def prep_chunks(first, end):
        n = NT // CHUNKS

        def prep(t, carry):
            v = af[t]
            hi = v.astype(BF16)
            wt[t, 0] = hi
            wt[t, 1] = (v - hi.astype(F32)).astype(BF16)
            return carry

        for i in range(first, end):
            a_copy(i).wait()
            lax.fori_loop(i * n, (i + 1) * n, prep, 0, unroll=2)

    prep_chunks(0, CHUNKS // 2)
    pl.semaphore_wait(barrier, len(greeted))
    for h in both:
        for j in (2, 1, 3):
            ca_copy(h, j).start()
    for l in range(1, LEAD_MAX + 1):
        lag_copy(l).start()
    prep_chunks(CHUNKS // 2, CHUNKS)

    def products(h, src, o_src, o_prev, forward):
        def pair(p, carry):
            ts = (2 * p, 2 * p + 1)
            rows = []
            for t in ts:
                rows += split(src[tab[o_src + t]])
            lhs = jnp.concatenate(rows, axis=0).astype(BF16)
            lhs = jnp.concatenate([lhs, lhs], axis=1)
            (h1, l1), (h2, l2) = [(wt[t, 0], wt[t, 1]) for t in ts]
            if forward:
                quarters, contract = (h1, l1, h2, l2), 1
            else:
                quarters, contract = (h1, h2, l1, l2), 0
            w = jnp.concatenate(
                [jnp.concatenate(quarters[:2], axis=1), jnp.concatenate(quarters[2:], axis=1)], axis=0
            )
            out = lax.dot_general(lhs, w, (((1,), (contract,)), ((), ())), preferred_element_type=F32)
            for i, t in enumerate(ts):
                at, lanes = 16 * i, slice(i * T, (i + 1) * T)
                s_buf[h][t] = out[at:at + 8, lanes] + out[at + 8:at + 16, lanes] + s_buf[h][tab[o_prev + t]]
            return carry

        lax.fori_loop(0, NT // 2, pair, 0, unroll=16)

    def place(h, c, g, stat):
        if c == 0:
            pb[h, c, g, 0] = stat

        def one(i, carry):
            pb[h, c, g, 1 + i] = s_buf[h][tab[O_LC + c * 128 + g * 32 + i]]
            return carry

        lax.fori_loop(0, 32, one, 0, unroll=16)

    def start_ring(h, stat):
        for which, copies in ((3, (0, 1)), (1, (2,)), (2, (3,)), (0, ())):
            for c in range(2):
                place(h, c, ring(c)[which], stat)
                for i in copies:
                    rz_copy(h, c, i).start()

    def relay_ring(h):
        for c in range(2):
            g, up, dn, opp = ring(c)
            for side, block in ((0, up), (1, dn)):
                rz_copy(h, c, side).wait_recv()
                at, n = half_of(c, side)
                here = pl.ds(at, n)
                pb[h, c, block, here] = pb[h, c, block, here] + fb[h, c, side, 0:n]
                rz_copy(h, c, 4 + side).start()

    def start_plane(h):
        for c in range(2):
            for i in (2, 3, 4, 5):
                rz_copy(h, c, i).wait_recv()

            def ring_sum(i):
                return pb[h, c, g_of[c], i] + rb[h, c, 0, i] + rb[h, c, 1, i]

            for m in range(8):
                for k in range(4):
                    qb[h, c, m, 1 + k] = ring_sum(1 + m * 4 + k)
            if c == 0:
                stat = ring_sum(0)
                for m in range(8):
                    qb[h, c, m, 0] = stat
            for j in (4, 3, 5, 2, 6, 1, 7):
                rp_copy(h, c, j).start()

    def new_weight(old, sums, at):
        psq, dsq = [
            jnp.sum(jnp.where(lane == at + e, sums, 0.0), axis=1, keepdims=True) for e in range(2)
        ]
        return jnp.sqrt(old * jnp.sqrt((psq + epsilon) / (dsq + epsilon)))

    def lanes_sum(v):
        return jnp.sum(v, axis=1, keepdims=True)

    def update(h, it):
        square = zero
        for c in range(2):
            m = m_of[c]
            for j in range(1, 8):
                rp_copy(h, c, j).wait_recv()

            def total(k):
                return qb[h, c, m, k] + sum(tb[h, c, j, k] for j in range(7))

            if c == 0:
                old = wgt[h]
                wgt[h] = jnp.where(it > 0, new_weight(old, total(0), 0), old)
            pstep = step_scale / wgt[h]
            for kk in range(4):
                k = c * 4 + kk
                primal = pr[h, k]
                new = jnp.maximum(primal - pstep * (cost[k:k + 1, :] - total(1 + kk)), 0.0)
                change = new - primal
                square = square + change * change
                pr[h, k] = new
                xg[h][c * 128 + g_of[c] * 32 + m * 4 + kk] = 2.0 * new - primal
            for j in (4, 3, 5, 2, 6, 1, 7):
                ap_copy(h, c, j).start()
        yb[h, 1 - core, 16] = square
        yb[h, core, 16] = square

    def start_spread(h):
        for c in range(2):
            for j in range(1, 8):
                ap_copy(h, c, j, True).wait_recv()
            for i in range(4):
                az_copy(h, c, i).start()

    def relay_spread(h):
        for c in range(2):
            for i in range(2):
                az_copy(h, c, i, True).wait_recv()
                az_copy(h, c, 4 + i).start()

    def iteration(it, carry):
        for h in both:
            @pl.when(it == 0)
            def _():
                for j in range(1, 4):
                    ca_recv(h, j).wait_recv()

            @pl.when(it > 0)
            def _():
                prices_copy(h, True).wait_recv()

            products(h, dg[h], O_ROW, O_PC, False)
            start_ring(h, jnp.where(lane == 0, dg[h][16], dg[h][16] + dg[h][33]))
        for h in both:
            relay_ring(h)
        for h in both:
            start_plane(h)
        for h in both:
            update(h, it)
        for h in both:
            start_spread(h)
        for h in both:
            relay_spread(h)

        @pl.when(it == 0)
        def _():
            for l in range(1, LEAD_MAX + 1):
                lag_copy(l).wait_recv()
            for h in both:
                rows = slice(8 * h, 8 * h + 8)
                for k in range(8):
                    lanes = slice(k * T, (k + 1) * T)
                    periods = jnp.broadcast_to(lead[k:k + 1, :], (8, T))
                    lagged = jnp.zeros((8, T), F32)
                    for l in range(1, LEAD_MAX + 1):
                        lagged = jnp.where(periods == l, lag[l - 1, rows, lanes], lagged)
                    rhs[h, chip * 8 + k] = dem[rows, lanes] - return_share * lagged
                rhs_copy(h).start()
            for l in range(1, LEAD_MAX + 1):
                lag_copy(l).wait_send()

        for h in both:
            for c in range(2):
                for i in (2, 3, 4, 5):
                    az_copy(h, c, i, True).wait_recv()
            products(h, xg[h], O_C, O_PR, True)
            for r in range(RT):
                yb[h, r // 8 % 2, r // 16 * 8 + r % 8] = s_buf[h][tab[O_LR + r]]
            terms_copy(h).start()
        for h in both:
            terms_copy(h).wait_recv()
            ych[h] = yb[h, core] + yc[h]
            sums_copy(h, it).start()
        for h in both:
            @pl.when(it == 0)
            def _():
                rhs_copy(h, True).wait_recv()
                rhs_copy(h).wait_send()
                for j in range(1, 4):
                    ca_copy(h, j).wait_send()

            @pl.when(it > 0)
            def _():
                prices_copy(h).wait_send()

            sums_copy(h, it).wait_recv()
            dstep = step_scale * wgt[h]
            square = zero
            for k in range(16):
                push = ych[h, k] + yx[h, it, k]
                old = dg[h][core * 17 + k]
                new = old + dstep * (rhs[h, k] - push)
                change = new - old
                square = square + change * change
                dg[h][core * 17 + k] = new
            primal_square = lanes_sum(ych[h, 16] + yx[h, it, 16])
            dg[h][core * 17 + 16] = jnp.where(
                lane == 0, primal_square, jnp.where(lane == 1, lanes_sum(square), 0.0)
            )

            @pl.when(it < ITERS - 1)
            def _():
                prices_copy(h).start()

        for h in both:
            for c in range(2):
                for i in range(6):
                    rz_copy(h, c, i).wait_send()
                    az_copy(h, c, i).wait_send()
                for j in range(1, 8):
                    rp_copy(h, c, j).wait_send()
                    ap_copy(h, c, j).wait_send()
            terms_copy(h).wait_send()
            sums_copy(h, it).wait_send()
        return carry

    lax.fori_loop(0, ITERS, iteration, 0)

    packed = zero
    for h in both:
        stat = dg[h][core * 17 + 16]
        for e in range(2):
            value = lanes_sum(jnp.where(lane == e, stat, 0.0))
            packed = jnp.where(lane == 2 * h + e, value, packed)
    fs[0] = packed
    first = rc(fs.at[0], fc, fi_s.at[31], fi_r.at[31], b, other_core)
    first.start()
    for h in both:
        for k in range(8):
            prim_out[8 * h:8 * h + 8, k * T:(k + 1) * T] = pr[h, k]
            dual_out[8 * h:8 * h + 8, k * T:(k + 1) * T] = dg[h][core * 17 + chip * 8 + k]
    first.wait_recv()
    fs[1] = jnp.where(lane % 2 == 0, packed, packed + fc[...])
    copies = [rc(fs.at[1], fa.at[i], fi_s.at[i], fi_r.at[i], *to) for i, to in enumerate(band)]
    for c in copies:
        c.start()
    for c in copies:
        c.wait_recv()
    sums = fs[1] + jnp.sum(fa[...], axis=0)
    for h in both:
        w_out[8 * h:8 * h + 8, :] = new_weight(wgt[h], sums, 2 * h)
    first.wait_send()
    for c in copies:
        c.wait_send()


def on_device(
    demand, lead_periods, matrix_tiles, tile_pos, cost_vector, primal_init, dual_init, weight_init
):
    table = index_table(tile_pos)
    vmem = pl.BlockSpec(memory_space=pltpu.VMEM)
    smem = pl.BlockSpec(memory_space=pltpu.SMEM)
    hbm = pl.BlockSpec(memory_space=pl.ANY)
    dma = pltpu.SemaphoreType.DMA

    def buf(*shape, dtype=F32):
        return pltpu.VMEM(shape, dtype)

    primal, dual, weight = pl.pallas_call(
        kernel,
        out_shape=(
            jax.ShapeDtypeStruct((16, 1024), F32),
            jax.ShapeDtypeStruct((16, 1024), F32),
            jax.ShapeDtypeStruct((16, T), F32),
        ),
        in_specs=[smem, smem] + [hbm] * 6,
        out_specs=(vmem, vmem, vmem),
        scratch_shapes=[
            buf(16, 1024),
            buf(8, T, dtype=jnp.int32),
            buf(8, T),
            buf(16, 1024),
            buf(16, 1024),
            buf(NT, T, T),
            buf(NT, 2, T, T, dtype=BF16),
            buf(NT + 1, 8, T),
            buf(NT + 1, 8, T),
            buf(CT, 8, T),
            buf(CT, 8, T),
            buf(2, 2, 4, 33, 8, T),
            buf(2, 2, 2, 17, 8, T),
            buf(2, 2, 2, 33, 8, T),
            buf(2, 2, 8, 5, 8, T),
            buf(2, 2, 7, 5, 8, T),
            buf(34, 8, T),
            buf(34, 8, T),
            buf(2, 2, 17, 8, T),
            buf(2, 17, 8, T),
            buf(2, 17, 8, T),
            buf(2, ITERS, 17, 8, T),
            buf(2, 8, 8, T),
            buf(2, 16, 8, T),
            buf(4, 16, 1024),
            buf(2, 8, T),
            buf(2, 8, T),
            buf(8, T),
            buf(31, 8, T),
            dma((5,)), dma((CHUNKS,)), dma((4,)), dma((4,)),
            dma((2, 3)), dma((2, 3)), dma((2, 2, 6)), dma((2, 2, 6)), dma((2, 2, 7)), dma((2, 2, 7)),
            dma((2, 2, 7)), dma((2, 2, 7)), dma((2, 2, 6)), dma((2, 2, 6)), dma((3, 2)), dma((3, 2)),
            dma((2, ITERS)), dma((2,)), dma((2,)), dma((32,)), dma((32,)),
        ],
        compiler_params=pltpu.CompilerParams(
            collective_id=0, has_side_effects=True, vmem_limit_bytes=60 * 2**20
        ),
    )(
        table,
        weight_init,
        demand.T,
        lead_periods.reshape(8, T),
        matrix_tiles.reshape(NT, T, T),
        cost_vector.reshape(8, T),
        primal_init.T,
        dual_init.T,
    )
    return primal.T, dual.T, weight[:, 0]


def solution(mesh):
    in_specs = (
        P(("band", "col"), None),
        P(("band", "col")),
        P("band", "col", None, None, None),
        P("band", "col", None),
        P(("band", "col")),
        P(("band", "col"), None),
        P(("band", "col"), None),
        P(),
    )
    out_specs = (P(("band", "col"), None), P(("band", "col"), None), P())
    return jax.shard_map(
        on_device, mesh=mesh, in_specs=in_specs, out_specs=out_specs, check_vma=False
    )
```

```python
import jax
import jax.numpy as jnp
from jax import lax
from jax.experimental import pallas as pl
from jax.experimental.pallas import tpu as pltpu
from jax.sharding import PartitionSpec as P

ITERS = 3
LEAD_MAX = 4
step_scale = 0.45
return_share = 0.6
epsilon = 1e-06

NT = 128
T = 128
CT = 256
RT = 32
F32 = jnp.float32
BF16 = jnp.bfloat16
CHUNKS = 16
MESH = pl.DeviceIdType.MESH

O_ROW, O_C, O_PC, O_PR, O_LC, O_LR = 0, 128, 256, 384, 512, 768


def index_table(pos):
    pos = pos.reshape(-1)
    t = jnp.arange(NT, dtype=jnp.int32)
    row, col = pos // CT, pos % CT

    def order(c):
        k, z, x, y = c % 8, (c // 8) % 4, (c // 32) % 2, c // 64
        kk = k % 4
        return jnp.where(k < 4, ((z * 4 + y) * 2 + x) * 4 + kk, 128 + ((y * 4 + z) * 2 + x) * 4 + kk)

    def prev(key):
        same = (key[:, None] == key[None, :]) & (t[:, None] < t[None, :])
        found = jnp.max(jnp.where(same, t[:, None], -1), axis=0)
        return jnp.where(found < 0, NT, found)

    def last(key, count):
        ids = jnp.arange(count, dtype=jnp.int32)
        found = jnp.max(jnp.where(key[:, None] == ids[None, :], t[:, None], -1), axis=0)
        return jnp.where(found < 0, NT, found)

    drow = (row // 8) % 2 * 17 + row // 16 * 8 + row % 8
    return jnp.concatenate(
        [drow, order(col), prev(col), prev(row), last(order(col), CT), last(row, RT)]
    )


def split(v):
    hi = v.astype(BF16).astype(F32)
    return hi, v - hi


def kernel(
    tab, w0, dem_in, lead_in, a_hbm, cost_in, prim_in, dual_in,
    prim_out, dual_out, w_out,
    dem, lead, cost, prim0, dual0,
    af, wt, s0, s1, xg0, xg1, pb, fb, rb, qb, tb, dg0, dg1, yb, yc, ych, yx, pr, rhs, lag, wgt, fs, fc, fa,
    in_sem, a_sem, lag_s, lag_r, ca_s, ca_r, rz_s, rz_r, rp_s, rp_r, ap_s, ap_r, az_s, az_r, col_s, col_r,
    sums_r, rh_s, rh_r, fi_s, fi_r,
):
    b = lax.axis_index("band")
    q = lax.axis_index("col")
    y, x, z = b // 8, (b // 4) % 2, b % 4
    xg, dg, s_buf = (xg0, xg1), (dg0, dg1), (s0, s1)
    both = range(2)

    def rc(src, dst, ss, rs, band, col):
        return pltpu.make_async_remote_copy(
            src_ref=src, dst_ref=dst, send_sem=ss, recv_sem=rs,
            device_id=(band, col), device_id_type=MESH,
        )

    g_of = (z, y)
    m_of = (y * 2 + x, z * 2 + x)

    def band_of(c, g, m):
        o, xx = m // 2, m % 2
        return o * 8 + xx * 4 + g if c == 0 else g * 8 + xx * 4 + o

    band = [((b + i) % 32, q) for i in range(1, 32)]
    core, chip = q % 2, q // 2
    other_core, other_chip = q + 1 - 2 * core, (q + 2) % 4

    def a_copy(i):
        n = NT // CHUNKS
        return pltpu.make_async_copy(a_hbm.at[pl.ds(i * n, n)], af.at[pl.ds(i * n, n)], a_sem.at[i])

    def lag_copy(l):
        return rc(dem, lag.at[l - 1], lag_s.at[l - 1], lag_r.at[l - 1], (b + l) % 32, q)

    def ca_copy(h, j):
        own = dg[h].at[pl.ds(core * 17 + chip * 8, 8)]
        return rc(own, own, ca_s.at[h, j - 1], ca_r.at[h, j - 1], b, (q + j) % 4)

    def ca_recv(h, j):
        q2 = (q + 4 - j) % 4
        slot = dg[h].at[pl.ds(q2 % 2 * 17 + q2 // 2 * 8, 8)]
        return rc(slot, slot, ca_s.at[h, j - 1], ca_r.at[h, j - 1], b, q2)

    def terms_copy(h):
        return rc(yb.at[h, 1 - core], yc.at[h], col_s.at[0, h], col_r.at[0, h], b, other_core)

    def sums_copy(h, it):
        return rc(ych.at[h], yx.at[h, it], col_s.at[1, h], sums_r.at[h, it], b, other_chip)

    def prices_copy(h, back=False):
        slot = dg[h].at[pl.ds((1 - core if back else core) * 17, 17)]
        return rc(slot, slot, col_s.at[2, h], col_r.at[2, h], b, other_core)

    def rhs_copy(h, back=False):
        slot = rhs.at[h, pl.ds((1 - chip if back else chip) * 8, 8)]
        return rc(slot, slot, rh_s.at[h], rh_r.at[h], b, other_chip)

    def ring(c):
        g = g_of[c]
        return g, (g + 1) % 4, (g + 3) % 4, (g + 2) % 4

    def half_of(c, half):
        return (17, 16) if half else (c, 17 - c)

    def rz_copy(h, c, i):
        g, up, dn, opp = ring(c)
        block, side, half = ((opp, 0, 0), (opp, 1, 1), (up, 0, 1), (dn, 1, 0), (up, 0, 0), (dn, 1, 1))[i]
        at, n = half_of(c, half)
        src = pb.at[h, c, block, pl.ds(at, n)]
        dst = fb.at[h, c, side, pl.ds(0, n)] if i < 2 else rb.at[h, c, side, pl.ds(at, n)]
        return rc(
            src, dst, rz_s.at[h, c, i], rz_r.at[h, c, i], band_of(c, dn if side else up, m_of[c]), q
        )

    def rp_copy(h, c, j):
        m2 = (m_of[c] + j) % 8
        part = pl.ds(1, 4) if c else pl.ds(0, 5)
        return rc(
            qb.at[h, c, m2, part], tb.at[h, c, j - 1, part], rp_s.at[h, c, j - 1], rp_r.at[h, c, j - 1],
            band_of(c, g_of[c], m2), q,
        )

    def ap_copy(h, c, j, back=False):
        m = m_of[c]
        m2 = (m + 8 - j) % 8 if back else (m + j) % 8
        slot = xg[h].at[pl.ds(c * 128 + g_of[c] * 32 + (m2 if back else m) * 4, 4)]
        return rc(slot, slot, ap_s.at[h, c, j - 1], ap_r.at[h, c, j - 1], band_of(c, g_of[c], m2), q)

    def az_copy(h, c, i, back=False):
        g, up, dn, opp = ring(c)
        lo, hi = (dn, up) if back else (g, g)
        block, half = (
            (lo, 0), (hi, 1), (lo, 1), (hi, 0), (opp if back else dn, 0), (opp if back else up, 1)
        )[i]
        slot = xg[h].at[pl.ds(c * 128 + block * 32 + half * 16, 16)]
        to = band_of(c, dn if i % 2 else up, m_of[c])
        return rc(slot, slot, az_s.at[h, c, i], az_r.at[h, c, i], to, q)

    inputs = [
        pltpu.make_async_copy(src, dst, in_sem.at[i])
        for i, (src, dst) in enumerate(
            ((dual_in, dual0), (dem_in, dem), (prim_in, prim0), (cost_in, cost), (lead_in, lead))
        )
    ]
    for c in inputs:
        c.start()
    for i in range(CHUNKS):
        a_copy(i).start()
    greeted = band + [(b, (q + j) % 4) for j in (1, 2, 3)]
    barrier = pltpu.get_barrier_semaphore()
    for to in greeted:
        pl.semaphore_signal(barrier, inc=1, device_id=to, device_id_type=MESH)
    zero = jnp.zeros((8, T), F32)
    sublane = lax.broadcasted_iota(jnp.int32, (8, T), 0)
    lane = lax.broadcasted_iota(jnp.int32, (8, T), 1)
    for c in inputs:
        c.wait()
    for h in both:
        for k in range(8):
            dg[h][core * 17 + chip * 8 + k] = dual0[8 * h:8 * h + 8, k * T:(k + 1) * T]
            pr[h, k] = prim0[8 * h:8 * h + 8, k * T:(k + 1) * T]
        dg[h][16] = zero
        dg[h][33] = zero
        weight = zero
        for i in range(8):
            weight = jnp.where(sublane == i, w0[8 * h + i], weight)
        wgt[h] = weight
        s_buf[h][NT] = zero

    def prep_chunks(first, end):
        n = NT // CHUNKS

        def prep(t, carry):
            v = af[t]
            hi = v.astype(BF16)
            wt[t, 0] = hi
            wt[t, 1] = (v - hi.astype(F32)).astype(BF16)
            return carry

        for i in range(first, end):
            a_copy(i).wait()
            lax.fori_loop(i * n, (i + 1) * n, prep, 0, unroll=2)

    prep_chunks(0, CHUNKS // 2)
    pl.semaphore_wait(barrier, len(greeted))
    for h in both:
        for j in (2, 1, 3):
            ca_copy(h, j).start()
    for l in range(1, LEAD_MAX + 1):
        lag_copy(l).start()
    prep_chunks(CHUNKS // 2, CHUNKS)

    def products(h, src, o_src, o_prev, forward, between=None, at=48):
        def pair(p, carry):
            ts = (2 * p, 2 * p + 1)
            rows = []
            for t in ts:
                rows += split(src[tab[o_src + t]])
            lhs = jnp.concatenate(rows, axis=0).astype(BF16)
            lhs = jnp.concatenate([lhs, lhs], axis=1)
            (h1, l1), (h2, l2) = [(wt[t, 0], wt[t, 1]) for t in ts]
            if forward:
                quarters, contract = (h1, l1, h2, l2), 1
            else:
                quarters, contract = (h1, h2, l1, l2), 0
            w = jnp.concatenate(
                [jnp.concatenate(quarters[:2], axis=1), jnp.concatenate(quarters[2:], axis=1)], axis=0
            )
            out = lax.dot_general(lhs, w, (((1,), (contract,)), ((), ())), preferred_element_type=F32)
            for i, t in enumerate(ts):
                row, lanes = 16 * i, slice(i * T, (i + 1) * T)
                s_buf[h][t] = out[row:row + 8, lanes] + out[row + 8:row + 16, lanes] + s_buf[h][tab[o_prev + t]]
            return carry

        lax.fori_loop(0, at, pair, 0, unroll=16)
        if between:
            between()
        lax.fori_loop(at, NT // 2, pair, 0, unroll=16)

    def place(h, c, g, stat):
        if c == 0:
            pb[h, c, g, 0] = stat

        def one(i, carry):
            pb[h, c, g, 1 + i] = s_buf[h][tab[O_LC + c * 128 + g * 32 + i]]
            return carry

        lax.fori_loop(0, 32, one, 0, unroll=16)

    def start_ring(h, stat):
        for which, copies in ((3, (0, 1)), (1, (2,)), (2, (3,)), (0, ())):
            for c in range(2):
                place(h, c, ring(c)[which], stat)
                for i in copies:
                    rz_copy(h, c, i).start()

    def relay_ring(h):
        for c in range(2):
            g, up, dn, opp = ring(c)
            for side, block in ((0, up), (1, dn)):
                rz_copy(h, c, side).wait_recv()
                at, n = half_of(c, side)
                here = pl.ds(at, n)
                pb[h, c, block, here] = pb[h, c, block, here] + fb[h, c, side, 0:n]
                rz_copy(h, c, 4 + side).start()

    def start_plane(h):
        for c in range(2):
            for i in (2, 3, 4, 5):
                rz_copy(h, c, i).wait_recv()

            def ring_sum(i):
                return pb[h, c, g_of[c], i] + rb[h, c, 0, i] + rb[h, c, 1, i]

            for m in range(8):
                for k in range(4):
                    qb[h, c, m, 1 + k] = ring_sum(1 + m * 4 + k)
            if c == 0:
                stat = ring_sum(0)
                for m in range(8):
                    qb[h, c, m, 0] = stat
            for j in (4, 3, 5, 2, 6, 1, 7):
                rp_copy(h, c, j).start()

    def new_weight(old, sums, at):
        psq, dsq = [
            jnp.sum(jnp.where(lane == at + e, sums, 0.0), axis=1, keepdims=True) for e in range(2)
        ]
        return jnp.sqrt(old * jnp.sqrt((psq + epsilon) / (dsq + epsilon)))

    def lanes_sum(v):
        return jnp.sum(v, axis=1, keepdims=True)

    def update(h, it):
        square = zero
        for c in range(2):
            m = m_of[c]
            for j in range(1, 8):
                rp_copy(h, c, j).wait_recv()

            def total(k):
                return qb[h, c, m, k] + sum(tb[h, c, j, k] for j in range(7))

            if c == 0:
                old = wgt[h]
                wgt[h] = jnp.where(it > 0, new_weight(old, total(0), 0), old)
            pstep = step_scale / wgt[h]
            for kk in range(4):
                k = c * 4 + kk
                primal = pr[h, k]
                new = jnp.maximum(primal - pstep * (cost[k:k + 1, :] - total(1 + kk)), 0.0)
                change = new - primal
                square = square + change * change
                pr[h, k] = new
                xg[h][c * 128 + g_of[c] * 32 + m * 4 + kk] = 2.0 * new - primal
            for j in (4, 3, 5, 2, 6, 1, 7):
                ap_copy(h, c, j).start()
        yb[h, 1 - core, 16] = square
        yb[h, core, 16] = square

    def start_spread(h):
        for c in range(2):
            for j in range(1, 8):
                ap_copy(h, c, j, True).wait_recv()
            for i in range(4):
                az_copy(h, c, i).start()

    def relay_spread(h):
        for c in range(2):
            for i in range(2):
                az_copy(h, c, i, True).wait_recv()
                az_copy(h, c, 4 + i).start()

    def transposed(h, between=None):
        products(h, dg[h], O_ROW, O_PC, False, between)
        start_ring(h, jnp.where(lane == 0, dg[h][16], dg[h][16] + dg[h][33]))

    def send_sums(h, it):
        terms_copy(h).wait_recv()
        ych[h] = yb[h, core] + yc[h]
        sums_copy(h, it).start()

    def dual_update(h, it):
        @pl.when(it == 0)
        def _():
            rhs_copy(h, True).wait_recv()
            rhs_copy(h).wait_send()
            for j in range(1, 4):
                ca_copy(h, j).wait_send()

        @pl.when(it > 0)
        def _():
            prices_copy(h).wait_send()

        sums_copy(h, it).wait_recv()
        dstep = step_scale * wgt[h]
        square = zero
        for k in range(16):
            push = ych[h, k] + yx[h, it, k]
            old = dg[h][core * 17 + k]
            new = old + dstep * (rhs[h, k] - push)
            change = new - old
            square = square + change * change
            dg[h][core * 17 + k] = new
        primal_square = lanes_sum(ych[h, 16] + yx[h, it, 16])
        dg[h][core * 17 + 16] = jnp.where(
            lane == 0, primal_square, jnp.where(lane == 1, lanes_sum(square), 0.0)
        )

    def iteration(it, carry):
        @pl.when(it == 0)
        def _():
            for j in range(1, 4):
                ca_recv(1, j).wait_recv()

        @pl.when(it > 0)
        def _():
            prices_copy(1, True).wait_recv()

        transposed(1)
        for h in both:
            relay_ring(h)
        for h in both:
            start_plane(h)
        for h in both:
            update(h, it)
        for h in both:
            start_spread(h)
        for h in both:
            relay_spread(h)

        @pl.when(it == 0)
        def _():
            for l in range(1, LEAD_MAX + 1):
                lag_copy(l).wait_recv()
            for h in both:
                rows = slice(8 * h, 8 * h + 8)
                for k in range(8):
                    lanes = slice(k * T, (k + 1) * T)
                    periods = jnp.broadcast_to(lead[k:k + 1, :], (8, T))
                    lagged = jnp.zeros((8, T), F32)
                    for l in range(1, LEAD_MAX + 1):
                        lagged = jnp.where(periods == l, lag[l - 1, rows, lanes], lagged)
                    rhs[h, chip * 8 + k] = dem[rows, lanes] - return_share * lagged
                rhs_copy(h).start()
            for l in range(1, LEAD_MAX + 1):
                lag_copy(l).wait_send()

        for h in both:
            for c in range(2):
                for i in (2, 3, 4, 5):
                    az_copy(h, c, i, True).wait_recv()
            products(h, xg[h], O_C, O_PR, True, (lambda: send_sums(0, it)) if h else None)
            for r in range(RT):
                yb[h, r // 8 % 2, r // 16 * 8 + r % 8] = s_buf[h][tab[O_LR + r]]
            terms_copy(h).start()
        send_sums(1, it)
        for h in both:
            for c in range(2):
                for i in range(6):
                    rz_copy(h, c, i).wait_send()
                    az_copy(h, c, i).wait_send()
                for j in range(1, 8):
                    rp_copy(h, c, j).wait_send()
                    ap_copy(h, c, j).wait_send()
            terms_copy(h).wait_send()
        dual_update(0, it)

        @pl.when(it < ITERS - 1)
        def _():
            prices_copy(0).start()
            prices_copy(0, True).wait_recv()

            def other_half():
                dual_update(1, it)
                prices_copy(1).start()

            transposed(0, other_half)

        @pl.when(it == ITERS - 1)
        def _():
            dual_update(1, it)

        for h in both:
            sums_copy(h, it).wait_send()
        return carry

    for j in range(1, 4):
        ca_recv(0, j).wait_recv()
    transposed(0)
    lax.fori_loop(0, ITERS, iteration, 0)

    packed = zero
    for h in both:
        stat = dg[h][core * 17 + 16]
        for e in range(2):
            value = lanes_sum(jnp.where(lane == e, stat, 0.0))
            packed = jnp.where(lane == 2 * h + e, value, packed)
    fs[0] = packed
    first = rc(fs.at[0], fc, fi_s.at[31], fi_r.at[31], b, other_core)
    first.start()
    for h in both:
        for k in range(8):
            prim_out[8 * h:8 * h + 8, k * T:(k + 1) * T] = pr[h, k]
            dual_out[8 * h:8 * h + 8, k * T:(k + 1) * T] = dg[h][core * 17 + chip * 8 + k]
    first.wait_recv()
    fs[1] = jnp.where(lane % 2 == 0, packed, packed + fc[...])
    copies = [rc(fs.at[1], fa.at[i], fi_s.at[i], fi_r.at[i], *to) for i, to in enumerate(band)]
    for c in copies:
        c.start()
    for c in copies:
        c.wait_recv()
    sums = fs[1] + jnp.sum(fa[...], axis=0)
    for h in both:
        w_out[8 * h:8 * h + 8, :] = new_weight(wgt[h], sums, 2 * h)
    first.wait_send()
    for c in copies:
        c.wait_send()


def on_device(
    demand, lead_periods, matrix_tiles, tile_pos, cost_vector, primal_init, dual_init, weight_init
):
    table = index_table(tile_pos)
    vmem = pl.BlockSpec(memory_space=pltpu.VMEM)
    smem = pl.BlockSpec(memory_space=pltpu.SMEM)
    hbm = pl.BlockSpec(memory_space=pl.ANY)
    dma = pltpu.SemaphoreType.DMA

    def buf(*shape, dtype=F32):
        return pltpu.VMEM(shape, dtype)

    primal, dual, weight = pl.pallas_call(
        kernel,
        out_shape=(
            jax.ShapeDtypeStruct((16, 1024), F32),
            jax.ShapeDtypeStruct((16, 1024), F32),
            jax.ShapeDtypeStruct((16, T), F32),
        ),
        in_specs=[smem, smem] + [hbm] * 6,
        out_specs=(vmem, vmem, vmem),
        scratch_shapes=[
            buf(16, 1024),
            buf(8, T, dtype=jnp.int32),
            buf(8, T),
            buf(16, 1024),
            buf(16, 1024),
            buf(NT, T, T),
            buf(NT, 2, T, T, dtype=BF16),
            buf(NT + 1, 8, T),
            buf(NT + 1, 8, T),
            buf(CT, 8, T),
            buf(CT, 8, T),
            buf(2, 2, 4, 33, 8, T),
            buf(2, 2, 2, 17, 8, T),
            buf(2, 2, 2, 33, 8, T),
            buf(2, 2, 8, 5, 8, T),
            buf(2, 2, 7, 5, 8, T),
            buf(34, 8, T),
            buf(34, 8, T),
            buf(2, 2, 17, 8, T),
            buf(2, 17, 8, T),
            buf(2, 17, 8, T),
            buf(2, ITERS, 17, 8, T),
            buf(2, 8, 8, T),
            buf(2, 16, 8, T),
            buf(4, 16, 1024),
            buf(2, 8, T),
            buf(2, 8, T),
            buf(8, T),
            buf(31, 8, T),
            dma((5,)), dma((CHUNKS,)), dma((4,)), dma((4,)),
            dma((2, 3)), dma((2, 3)), dma((2, 2, 6)), dma((2, 2, 6)), dma((2, 2, 7)), dma((2, 2, 7)),
            dma((2, 2, 7)), dma((2, 2, 7)), dma((2, 2, 6)), dma((2, 2, 6)), dma((3, 2)), dma((3, 2)),
            dma((2, ITERS)), dma((2,)), dma((2,)), dma((32,)), dma((32,)),
        ],
        compiler_params=pltpu.CompilerParams(
            collective_id=0, has_side_effects=True, vmem_limit_bytes=60 * 2**20
        ),
    )(
        table,
        weight_init,
        demand.T,
        lead_periods.reshape(8, T),
        matrix_tiles.reshape(NT, T, T),
        cost_vector.reshape(8, T),
        primal_init.T,
        dual_init.T,
    )
    return primal.T, dual.T, weight[:, 0]


def solution(mesh):
    in_specs = (
        P(("band", "col"), None),
        P(("band", "col")),
        P("band", "col", None, None, None),
        P("band", "col", None),
        P(("band", "col")),
        P(("band", "col"), None),
        P(("band", "col"), None),
        P(),
    )
    out_specs = (P(("band", "col"), None), P(("band", "col"), None), P())
    return jax.shard_map(
        on_device, mesh=mesh, in_specs=in_specs, out_specs=out_specs, check_vma=False
    )
```

```python
import jax
import jax.numpy as jnp
from jax import lax
from jax.experimental import pallas as pl
from jax.experimental.pallas import tpu as pltpu
from jax.sharding import PartitionSpec as P

ITERS = 3
LEAD_MAX = 4
step_scale = 0.45
return_share = 0.6
epsilon = 1e-06

NT = 128
T = 128
CT = 256
RT = 32
F32 = jnp.float32
BF16 = jnp.bfloat16
CHUNKS = 16
MESH = pl.DeviceIdType.MESH

ROW, COL, PREV_COL, PREV_ROW, LAST_COL, LAST_ROW = 0, 1, 2, 3, 4, 6


def index_table(pos):
    shift = lax.shift_right_logical
    here = jnp.broadcast_to(pos, (NT, NT))
    above = here.T
    u = lax.broadcasted_iota(jnp.int32, (NT, NT), 0)
    t = lax.broadcasted_iota(jnp.int32, (NT, NT), 1)

    def row(v):
        return shift(v, 8)

    def col(v):
        return v & 255

    def row_place(v):
        r = row(v)
        return (shift(r, 3) & 1) * 17 + shift(r, 4) * 8 + (r & 7)

    def col_place(v):
        k, z, x, y = v & 7, shift(v, 3) & 3, shift(v, 5) & 1, shift(col(v), 6)
        kk = k & 3
        return jnp.where(k < 4, z * 32 + y * 8 + x * 4 + kk, 128 + y * 32 + z * 8 + x * 4 + kk)

    def latest(where):
        found = jnp.max(jnp.where(where, u, -1), axis=0, keepdims=True)
        return jnp.where(found < 0, NT, found)

    place = col_place(above)
    return [
        row_place(pos),
        col_place(pos),
        latest((col(above) == col(here)) & (u < t)),
        latest((row(above) == row(here)) & (u < t)),
        latest(place == t),
        latest(place == t + NT),
        latest(row(above) == t),
    ]


def split(v):
    hi = v.astype(BF16).astype(F32)
    return hi, v - hi


def kernel(
    w0, pos_in, dem_in, lead_in, a_hbm, cost_in, prim_in, dual_in,
    prim_out, dual_out, w_out,
    tab, tab_v, pos, dem, lead, cost, prim0, dual0,
    af, wt, wf, s0, s1, xg0, xg1, pb, fb, rb, qb, tb, dg0, dg1, yb, yc, ych, yx, pr, rhs, lag, wgt, fs, fc, fa,
    in_sem, a_sem, lag_s, lag_r, ca_s, ca_r, rz_s, rz_r, rp_s, rp_r, ap_s, ap_r, az_s, az_r, col_s, col_r,
    sums_r, rh_s, rh_r, fi_s, fi_r,
):
    b = lax.axis_index("band")
    q = lax.axis_index("col")
    y, x, z = b // 8, (b // 4) % 2, b % 4
    xg, dg, s_buf = (xg0, xg1), (dg0, dg1), (s0, s1)
    both = range(2)

    def rc(src, dst, ss, rs, band, col):
        return pltpu.make_async_remote_copy(
            src_ref=src, dst_ref=dst, send_sem=ss, recv_sem=rs,
            device_id=(band, col), device_id_type=MESH,
        )

    g_of = (z, y)
    m_of = (y * 2 + x, z * 2 + x)

    def band_of(c, g, m):
        o, xx = m // 2, m % 2
        return o * 8 + xx * 4 + g if c == 0 else g * 8 + xx * 4 + o

    band = [((b + i) % 32, q) for i in range(1, 32)]
    core, chip = q % 2, q // 2
    other_core, other_chip = q + 1 - 2 * core, (q + 2) % 4

    def a_copy(i):
        n = NT // CHUNKS
        return pltpu.make_async_copy(a_hbm.at[pl.ds(i * n, n)], af.at[pl.ds(i * n, n)], a_sem.at[i])

    def lag_copy(l):
        return rc(dem, lag.at[l - 1], lag_s.at[l - 1], lag_r.at[l - 1], (b + l) % 32, q)

    def ca_copy(h, j):
        own = dg[h].at[pl.ds(core * 17 + chip * 8, 8)]
        return rc(own, own, ca_s.at[h, j - 1], ca_r.at[h, j - 1], b, (q + j) % 4)

    def ca_recv(h, j):
        q2 = (q + 4 - j) % 4
        slot = dg[h].at[pl.ds(q2 % 2 * 17 + q2 // 2 * 8, 8)]
        return rc(slot, slot, ca_s.at[h, j - 1], ca_r.at[h, j - 1], b, q2)

    def terms_copy(h):
        return rc(yb.at[h, 1 - core], yc.at[h], col_s.at[0, h], col_r.at[0, h], b, other_core)

    def sums_copy(h, it):
        return rc(ych.at[h], yx.at[h, it], col_s.at[1, h], sums_r.at[h, it], b, other_chip)

    def prices_copy(h, back=False):
        slot = dg[h].at[pl.ds((1 - core if back else core) * 17, 17)]
        return rc(slot, slot, col_s.at[2, h], col_r.at[2, h], b, other_core)

    def rhs_copy(h, back=False):
        slot = rhs.at[h, pl.ds((1 - chip if back else chip) * 8, 8)]
        return rc(slot, slot, rh_s.at[h], rh_r.at[h], b, other_chip)

    def ring(c):
        g = g_of[c]
        return g, (g + 1) % 4, (g + 3) % 4, (g + 2) % 4

    def half_of(c, half):
        return (17, 16) if half else (c, 17 - c)

    def rz_copy(h, c, i):
        g, up, dn, opp = ring(c)
        block, side, half = ((opp, 0, 0), (opp, 1, 1), (up, 0, 1), (dn, 1, 0), (up, 0, 0), (dn, 1, 1))[i]
        at, n = half_of(c, half)
        src = pb.at[h, c, block, pl.ds(at, n)]
        dst = fb.at[h, c, side, pl.ds(0, n)] if i < 2 else rb.at[h, c, side, pl.ds(at, n)]
        return rc(
            src, dst, rz_s.at[h, c, i], rz_r.at[h, c, i], band_of(c, dn if side else up, m_of[c]), q
        )

    def rp_copy(h, c, j):
        m2 = (m_of[c] + j) % 8
        part = pl.ds(1, 4) if c else pl.ds(0, 5)
        return rc(
            qb.at[h, c, m2, part], tb.at[h, c, j - 1, part], rp_s.at[h, c, j - 1], rp_r.at[h, c, j - 1],
            band_of(c, g_of[c], m2), q,
        )

    def ap_copy(h, c, j, back=False):
        m = m_of[c]
        m2 = (m + 8 - j) % 8 if back else (m + j) % 8
        slot = xg[h].at[pl.ds(c * 128 + g_of[c] * 32 + (m2 if back else m) * 4, 4)]
        return rc(slot, slot, ap_s.at[h, c, j - 1], ap_r.at[h, c, j - 1], band_of(c, g_of[c], m2), q)

    def az_copy(h, c, i, back=False):
        g, up, dn, opp = ring(c)
        lo, hi = (dn, up) if back else (g, g)
        block, half = (
            (lo, 0), (hi, 1), (lo, 1), (hi, 0), (opp if back else dn, 0), (opp if back else up, 1)
        )[i]
        slot = xg[h].at[pl.ds(c * 128 + block * 32 + half * 16, 16)]
        to = band_of(c, dn if i % 2 else up, m_of[c])
        return rc(slot, slot, az_s.at[h, c, i], az_r.at[h, c, i], to, q)

    inputs = [
        pltpu.make_async_copy(src, dst, in_sem.at[i])
        for i, (src, dst) in enumerate(
            ((pos_in, pos), (dual_in, dual0), (dem_in, dem), (prim_in, prim0), (cost_in, cost), (lead_in, lead))
        )
    ]
    for c in inputs:
        c.start()
    for i in range(CHUNKS):
        a_copy(i).start()
    greeted = band + [(b, (q + j) % 4) for j in (1, 2, 3)]
    barrier = pltpu.get_barrier_semaphore()
    for to in greeted:
        pl.semaphore_signal(barrier, inc=1, device_id=to, device_id_type=MESH)
    zero = jnp.zeros((8, T), F32)
    sublane = lax.broadcasted_iota(jnp.int32, (8, T), 0)
    lane = lax.broadcasted_iota(jnp.int32, (8, T), 1)
    for c in inputs:
        c.wait()
    for h in both:
        for k in range(8):
            dg[h][core * 17 + chip * 8 + k] = dual0[8 * h:8 * h + 8, k * T:(k + 1) * T]
            pr[h, k] = prim0[8 * h:8 * h + 8, k * T:(k + 1) * T]
        dg[h][16] = zero
        dg[h][33] = zero
        weight = zero
        for i in range(8):
            weight = jnp.where(sublane == i, w0[8 * h + i], weight)
        wgt[h] = weight
        s_buf[h][NT] = zero

    tab_v[...] = jnp.zeros((8, NT), jnp.int32)
    for i, entry in enumerate(index_table(pos[...])):
        tab_v[i:i + 1, :] = entry
    table = pltpu.make_async_copy(tab_v, tab, in_sem.at[6])
    table.start()

    def prep_chunks(first, end):
        n = NT // CHUNKS

        def prep(t, carry):
            v = af[t]
            hi = v.astype(BF16)
            wt[t, 0] = hi
            wt[t, 1] = (v - hi.astype(F32)).astype(BF16)
            return carry

        for i in range(first, end):
            a_copy(i).wait()
            lax.fori_loop(i * n, (i + 1) * n, prep, 0, unroll=2)

    prep_chunks(0, CHUNKS // 2)
    table.wait()
    pl.semaphore_wait(barrier, len(greeted))
    for h in both:
        for j in (2, 1, 3):
            ca_copy(h, j).start()
    for l in range(1, LEAD_MAX + 1):
        lag_copy(l).start()
    prep_chunks(CHUNKS // 2, CHUNKS)

    def products(h, src, o_src, o_prev, forward, between=None, at=48):
        def pair(p, carry):
            ts = (2 * p, 2 * p + 1)
            rows = []
            for t in ts:
                rows += split(src[tab[o_src, t]])
            lhs = jnp.concatenate(rows, axis=0).astype(BF16)
            lhs = jnp.concatenate([lhs, lhs], axis=1)
            tiles = wf if forward else wt
            (h1, l1), (h2, l2) = [(tiles[t, 0], tiles[t, 1]) for t in ts]
            w = jnp.concatenate(
                [jnp.concatenate([h1, h2], axis=1), jnp.concatenate([l1, l2], axis=1)], axis=0
            )
            out = lax.dot_general(lhs, w, (((1,), (0,)), ((), ())), preferred_element_type=F32)
            for i, t in enumerate(ts):
                row, lanes = 16 * i, slice(i * T, (i + 1) * T)
                s_buf[h][t] = out[row:row + 8, lanes] + out[row + 8:row + 16, lanes] + s_buf[h][tab[o_prev, t]]
            return carry

        lax.fori_loop(0, at, pair, 0, unroll=16)
        if between:
            between()
        lax.fori_loop(at, NT // 2, pair, 0, unroll=16)

    def place(h, c, g, stat):
        if c == 0:
            pb[h, c, g, 0] = stat

        def one(i, carry):
            pb[h, c, g, 1 + i] = s_buf[h][tab[LAST_COL + c, g * 32 + i]]
            return carry

        lax.fori_loop(0, 32, one, 0, unroll=16)

    def start_ring(h, stat):
        for which, copies in ((3, (0, 1)), (1, (2,)), (2, (3,)), (0, ())):
            for c in range(2):
                place(h, c, ring(c)[which], stat)
                for i in copies:
                    rz_copy(h, c, i).start()

    def relay_ring(h):
        for c in range(2):
            g, up, dn, opp = ring(c)
            for side, block in ((0, up), (1, dn)):
                rz_copy(h, c, side).wait_recv()
                at, n = half_of(c, side)
                here = pl.ds(at, n)
                pb[h, c, block, here] = pb[h, c, block, here] + fb[h, c, side, 0:n]
                rz_copy(h, c, 4 + side).start()

    def start_plane(h):
        for c in range(2):
            for i in (2, 3, 4, 5):
                rz_copy(h, c, i).wait_recv()

            def ring_sum(i):
                return pb[h, c, g_of[c], i] + rb[h, c, 0, i] + rb[h, c, 1, i]

            for m in range(8):
                for k in range(4):
                    qb[h, c, m, 1 + k] = ring_sum(1 + m * 4 + k)
            if c == 0:
                stat = ring_sum(0)
                for m in range(8):
                    qb[h, c, m, 0] = stat
            for j in (4, 3, 5, 2, 6, 1, 7):
                rp_copy(h, c, j).start()

    def new_weight(old, sums, at):
        psq, dsq = [
            jnp.sum(jnp.where(lane == at + e, sums, 0.0), axis=1, keepdims=True) for e in range(2)
        ]
        return jnp.sqrt(old * jnp.sqrt((psq + epsilon) / (dsq + epsilon)))

    def lanes_sum(v):
        return jnp.sum(v, axis=1, keepdims=True)

    def update(h, it):
        square = zero
        for c in range(2):
            m = m_of[c]
            for j in range(1, 8):
                rp_copy(h, c, j).wait_recv()

            def total(k):
                return qb[h, c, m, k] + sum(tb[h, c, j, k] for j in range(7))

            if c == 0:
                old = wgt[h]
                wgt[h] = jnp.where(it > 0, new_weight(old, total(0), 0), old)
            pstep = step_scale / wgt[h]
            for kk in range(4):
                k = c * 4 + kk
                primal = pr[h, k]
                new = jnp.maximum(primal - pstep * (cost[k:k + 1, :] - total(1 + kk)), 0.0)
                change = new - primal
                square = square + change * change
                pr[h, k] = new
                xg[h][c * 128 + g_of[c] * 32 + m * 4 + kk] = 2.0 * new - primal
            for j in (4, 3, 5, 2, 6, 1, 7):
                ap_copy(h, c, j).start()
        yb[h, 1 - core, 16] = square
        yb[h, core, 16] = square

    def start_spread(h):
        for c in range(2):
            for j in range(1, 8):
                ap_copy(h, c, j, True).wait_recv()
            for i in range(4):
                az_copy(h, c, i).start()

    def relay_spread(h):
        for c in range(2):
            for i in range(2):
                az_copy(h, c, i, True).wait_recv()
                az_copy(h, c, 4 + i).start()

    def transposed(h, between=None):
        products(h, dg[h], ROW, PREV_COL, False, between)
        start_ring(h, jnp.where(lane == 0, dg[h][16], dg[h][16] + dg[h][33]))

    def send_sums(h, it):
        terms_copy(h).wait_recv()
        ych[h] = yb[h, core] + yc[h]
        sums_copy(h, it).start()

    def dual_update(h, it):
        @pl.when(it == 0)
        def _():
            rhs_copy(h, True).wait_recv()
            rhs_copy(h).wait_send()
            for j in range(1, 4):
                ca_copy(h, j).wait_send()

        @pl.when(it > 0)
        def _():
            prices_copy(h).wait_send()

        sums_copy(h, it).wait_recv()
        dstep = step_scale * wgt[h]
        square = zero
        for k in range(16):
            push = ych[h, k] + yx[h, it, k]
            old = dg[h][core * 17 + k]
            new = old + dstep * (rhs[h, k] - push)
            change = new - old
            square = square + change * change
            dg[h][core * 17 + k] = new
        primal_square = lanes_sum(ych[h, 16] + yx[h, it, 16])
        dg[h][core * 17 + 16] = jnp.where(
            lane == 0, primal_square, jnp.where(lane == 1, lanes_sum(square), 0.0)
        )

    def turn(t, carry):
        v = af[t].T
        hi = v.astype(BF16)
        wf[t, 0] = hi
        wf[t, 1] = (v - hi.astype(F32)).astype(BF16)
        return carry

    def turn_some(it, first, end):
        @pl.when(it == 0)
        def _():
            lax.fori_loop(first, end, turn, 0, unroll=2)

    def iteration(it, carry):
        @pl.when(it == 0)
        def _():
            for j in range(1, 4):
                ca_recv(1, j).wait_recv()

        @pl.when(it > 0)
        def _():
            prices_copy(1, True).wait_recv()

        transposed(1)
        for h in both:
            relay_ring(h)

        turn_some(it, 0, 40)
        for h in both:
            start_plane(h)
        turn_some(it, 40, 88)
        for h in both:
            update(h, it)
        turn_some(it, 88, NT)
        for h in both:
            start_spread(h)
        for h in both:
            relay_spread(h)

        @pl.when(it == 0)
        def _():
            for l in range(1, LEAD_MAX + 1):
                lag_copy(l).wait_recv()
            for h in both:
                rows = slice(8 * h, 8 * h + 8)
                for k in range(8):
                    lanes = slice(k * T, (k + 1) * T)
                    periods = jnp.broadcast_to(lead[k:k + 1, :], (8, T))
                    lagged = jnp.zeros((8, T), F32)
                    for l in range(1, LEAD_MAX + 1):
                        lagged = jnp.where(periods == l, lag[l - 1, rows, lanes], lagged)
                    rhs[h, chip * 8 + k] = dem[rows, lanes] - return_share * lagged
                rhs_copy(h).start()
            for l in range(1, LEAD_MAX + 1):
                lag_copy(l).wait_send()

        for h in both:
            for c in range(2):
                for i in (2, 3, 4, 5):
                    az_copy(h, c, i, True).wait_recv()
            products(h, xg[h], COL, PREV_ROW, True, (lambda: send_sums(0, it)) if h else None)
            for r in range(RT):
                yb[h, r // 8 % 2, r // 16 * 8 + r % 8] = s_buf[h][tab[LAST_ROW, r]]
            terms_copy(h).start()
        send_sums(1, it)
        for h in both:
            for c in range(2):
                for i in range(6):
                    rz_copy(h, c, i).wait_send()
                    az_copy(h, c, i).wait_send()
                for j in range(1, 8):
                    rp_copy(h, c, j).wait_send()
                    ap_copy(h, c, j).wait_send()
            terms_copy(h).wait_send()
        dual_update(0, it)

        @pl.when(it < ITERS - 1)
        def _():
            prices_copy(0).start()
            prices_copy(0, True).wait_recv()

            def other_half():
                dual_update(1, it)
                prices_copy(1).start()

            transposed(0, other_half)

        @pl.when(it == ITERS - 1)
        def _():
            dual_update(1, it)

        for h in both:
            sums_copy(h, it).wait_send()
        return carry

    for j in range(1, 4):
        ca_recv(0, j).wait_recv()
    transposed(0)
    lax.fori_loop(0, ITERS, iteration, 0)

    packed = zero
    for h in both:
        stat = dg[h][core * 17 + 16]
        for e in range(2):
            value = lanes_sum(jnp.where(lane == e, stat, 0.0))
            packed = jnp.where(lane == 2 * h + e, value, packed)
    fs[0] = packed
    first = rc(fs.at[0], fc, fi_s.at[31], fi_r.at[31], b, other_core)
    first.start()
    for h in both:
        for k in range(8):
            prim_out[8 * h:8 * h + 8, k * T:(k + 1) * T] = pr[h, k]
            dual_out[8 * h:8 * h + 8, k * T:(k + 1) * T] = dg[h][core * 17 + chip * 8 + k]
    first.wait_recv()
    fs[1] = jnp.where(lane % 2 == 0, packed, packed + fc[...])
    copies = [rc(fs.at[1], fa.at[i], fi_s.at[i], fi_r.at[i], *to) for i, to in enumerate(band)]
    for c in copies:
        c.start()
    for c in copies:
        c.wait_recv()
    sums = fs[1] + jnp.sum(fa[...], axis=0)
    for h in both:
        w_out[8 * h:8 * h + 8, :] = new_weight(wgt[h], sums, 2 * h)
    first.wait_send()
    for c in copies:
        c.wait_send()


def on_device(
    demand, lead_periods, matrix_tiles, tile_pos, cost_vector, primal_init, dual_init, weight_init
):
    vmem = pl.BlockSpec(memory_space=pltpu.VMEM)
    smem = pl.BlockSpec(memory_space=pltpu.SMEM)
    hbm = pl.BlockSpec(memory_space=pl.ANY)
    dma = pltpu.SemaphoreType.DMA

    def buf(*shape, dtype=F32):
        return pltpu.VMEM(shape, dtype)

    primal, dual, weight = pl.pallas_call(
        kernel,
        out_shape=(
            jax.ShapeDtypeStruct((16, 1024), F32),
            jax.ShapeDtypeStruct((16, 1024), F32),
            jax.ShapeDtypeStruct((16, T), F32),
        ),
        in_specs=[smem] + [hbm] * 7,
        out_specs=(vmem, vmem, vmem),
        scratch_shapes=[
            pltpu.SMEM((8, NT), jnp.int32),
            buf(8, NT, dtype=jnp.int32),
            buf(1, NT, dtype=jnp.int32),
            buf(16, 1024),
            buf(8, T, dtype=jnp.int32),
            buf(8, T),
            buf(16, 1024),
            buf(16, 1024),
            buf(NT, T, T),
            buf(NT, 2, T, T, dtype=BF16),
            buf(NT, 2, T, T, dtype=BF16),
            buf(NT + 1, 8, T),
            buf(NT + 1, 8, T),
            buf(CT, 8, T),
            buf(CT, 8, T),
            buf(2, 2, 4, 33, 8, T),
            buf(2, 2, 2, 17, 8, T),
            buf(2, 2, 2, 33, 8, T),
            buf(2, 2, 8, 5, 8, T),
            buf(2, 2, 7, 5, 8, T),
            buf(34, 8, T),
            buf(34, 8, T),
            buf(2, 2, 17, 8, T),
            buf(2, 17, 8, T),
            buf(2, 17, 8, T),
            buf(2, ITERS, 17, 8, T),
            buf(2, 8, 8, T),
            buf(2, 16, 8, T),
            buf(4, 16, 1024),
            buf(2, 8, T),
            buf(2, 8, T),
            buf(8, T),
            buf(31, 8, T),
            dma((7,)), dma((CHUNKS,)), dma((4,)), dma((4,)),
            dma((2, 3)), dma((2, 3)), dma((2, 2, 6)), dma((2, 2, 6)), dma((2, 2, 7)), dma((2, 2, 7)),
            dma((2, 2, 7)), dma((2, 2, 7)), dma((2, 2, 6)), dma((2, 2, 6)), dma((3, 2)), dma((3, 2)),
            dma((2, ITERS)), dma((2,)), dma((2,)), dma((32,)), dma((32,)),
        ],
        compiler_params=pltpu.CompilerParams(
            collective_id=0, has_side_effects=True, vmem_limit_bytes=60 * 2**20
        ),
    )(
        weight_init,
        tile_pos.reshape(1, NT),
        demand.T,
        lead_periods.reshape(8, T),
        matrix_tiles.reshape(NT, T, T),
        cost_vector.reshape(8, T),
        primal_init.T,
        dual_init.T,
    )
    return primal.T, dual.T, weight[:, 0]


def solution(mesh):
    in_specs = (
        P(("band", "col"), None),
        P(("band", "col")),
        P("band", "col", None, None, None),
        P("band", "col", None),
        P(("band", "col")),
        P(("band", "col"), None),
        P(("band", "col"), None),
        P(),
    )
    out_specs = (P(("band", "col"), None), P(("band", "col"), None), P())
    return jax.shard_map(
        on_device, mesh=mesh, in_specs=in_specs, out_specs=out_specs, check_vma=False
    )
```

```python
import jax
import jax.numpy as jnp
from jax import lax
from jax.experimental import pallas as pl
from jax.experimental.pallas import tpu as pltpu
from jax.sharding import PartitionSpec as P

ITERS = 3
LEAD_MAX = 4
step_scale = 0.45
return_share = 0.6
epsilon = 1e-06

NT = 128
T = 128
CT = 256
RT = 32
F32 = jnp.float32
BF16 = jnp.bfloat16
CHUNKS = 16
MESH = pl.DeviceIdType.MESH

ROW, COL, PREV_COL, PREV_ROW, LAST_COL, LAST_ROW = 0, 1, 2, 3, 4, 6


def index_table(pos):
    shift = lax.shift_right_logical
    here = jnp.broadcast_to(pos, (NT, NT))
    above = here.T
    u = lax.broadcasted_iota(jnp.int32, (NT, NT), 0)
    t = lax.broadcasted_iota(jnp.int32, (NT, NT), 1)

    def row(v):
        return shift(v, 8)

    def col(v):
        return v & 255

    def row_place(v):
        r = row(v)
        return (shift(r, 3) & 1) * 17 + shift(r, 4) * 8 + (r & 7)

    def col_place(v):
        k, z, x, y = v & 7, shift(v, 3) & 3, shift(v, 5) & 1, shift(col(v), 6)
        kk = k & 3
        return jnp.where(k < 4, z * 32 + y * 8 + x * 4 + kk, 128 + y * 32 + z * 8 + x * 4 + kk)

    def latest(where):
        found = jnp.max(jnp.where(where, u, -1), axis=0, keepdims=True)
        return jnp.where(found < 0, NT, found)

    place = col_place(above)
    return [
        row_place(pos),
        col_place(pos),
        latest((col(above) == col(here)) & (u < t)),
        latest((row(above) == row(here)) & (u < t)),
        latest(place == t),
        latest(place == t + NT),
        latest(row(above) == t),
    ]


def split(v):
    hi = v.astype(BF16).astype(F32)
    return hi, v - hi


def kernel(
    w0, pos_in, dem_in, lead_in, a_hbm, cost_in, prim_in, dual_in,
    prim_out, dual_out, w_out,
    tab, tab_v, pos, dem, lead, cost, prim0, dual0,
    af, wt, wf, s0, s1, xg0, xg1, pb, fb, rb, qb, tb, dg0, dg1, yb, yc, ych, yx, pr, rhs, lag, wgt, fs, fc, fa,
    in_sem, a_sem, lag_s, lag_r, ca_s, ca_r, rz_s, rz_r, rp_s, rp_r, ap_s, ap_r, az_s, az_r, col_s, col_r,
    sums_r, rh_s, rh_r, fi_s, fi_r,
):
    b = lax.axis_index("band")
    q = lax.axis_index("col")
    y, x, z = b // 8, (b // 4) % 2, b % 4
    xg, dg, s_buf = (xg0, xg1), (dg0, dg1), (s0, s1)
    both = range(2)

    def rc(src, dst, ss, rs, band, col):
        return pltpu.make_async_remote_copy(
            src_ref=src, dst_ref=dst, send_sem=ss, recv_sem=rs,
            device_id=(band, col), device_id_type=MESH,
        )

    g_of = (z, y)
    m_of = (y * 2 + x, z * 2 + x)

    def band_of(c, g, m):
        o, xx = m // 2, m % 2
        return o * 8 + xx * 4 + g if c == 0 else g * 8 + xx * 4 + o

    band = [((b + i) % 32, q) for i in range(1, 32)]
    core, chip = q % 2, q // 2
    other_core, other_chip = q + 1 - 2 * core, (q + 2) % 4

    def a_copy(i):
        n = NT // CHUNKS
        return pltpu.make_async_copy(a_hbm.at[pl.ds(i * n, n)], af.at[pl.ds(i * n, n)], a_sem.at[i])

    def lag_copy(l):
        return rc(dem, lag.at[l - 1], lag_s.at[l - 1], lag_r.at[l - 1], (b + l) % 32, q)

    def ca_copy(h, j):
        own = dg[h].at[pl.ds(core * 17 + chip * 8, 8)]
        return rc(own, own, ca_s.at[h, j - 1], ca_r.at[h, j - 1], b, (q + j) % 4)

    def ca_recv(h, j):
        q2 = (q + 4 - j) % 4
        slot = dg[h].at[pl.ds(q2 % 2 * 17 + q2 // 2 * 8, 8)]
        return rc(slot, slot, ca_s.at[h, j - 1], ca_r.at[h, j - 1], b, q2)

    def terms_copy(h):
        return rc(yb.at[h, 1 - core], yc.at[h], col_s.at[0, h], col_r.at[0, h], b, other_core)

    def sums_copy(h, it):
        return rc(ych.at[h], yx.at[h, it], col_s.at[1, h], sums_r.at[h, it], b, other_chip)

    def prices_copy(h, back=False):
        slot = dg[h].at[pl.ds((1 - core if back else core) * 17, 17)]
        return rc(slot, slot, col_s.at[2, h], col_r.at[2, h], b, other_core)

    def rhs_copy(h, back=False):
        slot = rhs.at[h, pl.ds((1 - chip if back else chip) * 8, 8)]
        return rc(slot, slot, rh_s.at[h], rh_r.at[h], b, other_chip)

    def ring(c):
        g = g_of[c]
        return g, (g + 1) % 4, (g + 3) % 4, (g + 2) % 4

    def half_of(c, half):
        return (17, 16) if half else (c, 17 - c)

    def rz_copy(h, c, i):
        g, up, dn, opp = ring(c)
        block, side, half = ((opp, 0, 0), (opp, 1, 1), (up, 0, 1), (dn, 1, 0), (up, 0, 0), (dn, 1, 1))[i]
        at, n = half_of(c, half)
        src = pb.at[h, c, block, pl.ds(at, n)]
        dst = fb.at[h, c, side, pl.ds(0, n)] if i < 2 else rb.at[h, c, side, pl.ds(at, n)]
        return rc(
            src, dst, rz_s.at[h, c, i], rz_r.at[h, c, i], band_of(c, dn if side else up, m_of[c]), q
        )

    def rp_copy(h, c, j):
        m2 = (m_of[c] + j) % 8
        part = pl.ds(1, 4) if c else pl.ds(0, 5)
        return rc(
            qb.at[h, c, m2, part], tb.at[h, c, j - 1, part], rp_s.at[h, c, j - 1], rp_r.at[h, c, j - 1],
            band_of(c, g_of[c], m2), q,
        )

    def ap_copy(h, c, j, back=False):
        m = m_of[c]
        m2 = (m + 8 - j) % 8 if back else (m + j) % 8
        slot = xg[h].at[pl.ds(c * 128 + g_of[c] * 32 + (m2 if back else m) * 4, 4)]
        return rc(slot, slot, ap_s.at[h, c, j - 1], ap_r.at[h, c, j - 1], band_of(c, g_of[c], m2), q)

    def az_copy(h, c, i, back=False):
        g, up, dn, opp = ring(c)
        lo, hi = (dn, up) if back else (g, g)
        block, half = (
            (lo, 0), (hi, 1), (lo, 1), (hi, 0), (opp if back else dn, 0), (opp if back else up, 1)
        )[i]
        slot = xg[h].at[pl.ds(c * 128 + block * 32 + half * 16, 16)]
        to = band_of(c, dn if i % 2 else up, m_of[c])
        return rc(slot, slot, az_s.at[h, c, i], az_r.at[h, c, i], to, q)

    inputs = [
        pltpu.make_async_copy(src, dst, in_sem.at[i])
        for i, (src, dst) in enumerate(
            ((pos_in, pos), (dual_in, dual0), (dem_in, dem), (prim_in, prim0), (cost_in, cost), (lead_in, lead))
        )
    ]
    for c in inputs:
        c.start()
    for i in range(CHUNKS):
        a_copy(i).start()
    greeted = band + [(b, (q + j) % 4) for j in (1, 2, 3)]
    barrier = pltpu.get_barrier_semaphore()
    for to in greeted:
        pl.semaphore_signal(barrier, inc=1, device_id=to, device_id_type=MESH)
    zero = jnp.zeros((8, T), F32)
    sublane = lax.broadcasted_iota(jnp.int32, (8, T), 0)
    lane = lax.broadcasted_iota(jnp.int32, (8, T), 1)
    for c in inputs:
        c.wait()
    for h in both:
        for k in range(8):
            dg[h][core * 17 + chip * 8 + k] = dual0[8 * h:8 * h + 8, k * T:(k + 1) * T]
            pr[h, k] = prim0[8 * h:8 * h + 8, k * T:(k + 1) * T]
        dg[h][16] = zero
        dg[h][33] = zero
        weight = zero
        for i in range(8):
            weight = jnp.where(sublane == i, w0[8 * h + i], weight)
        wgt[h] = weight
        s_buf[h][NT] = zero

    tab_v[...] = jnp.zeros((8, NT), jnp.int32)
    for i, entry in enumerate(index_table(pos[...])):
        tab_v[i:i + 1, :] = entry
    table = pltpu.make_async_copy(tab_v, tab, in_sem.at[6])
    table.start()

    def prep_chunks(first, end):
        n = NT // CHUNKS

        def prep(t, carry):
            v = af[t]
            hi = v.astype(BF16)
            wt[t, 0] = hi
            wt[t, 1] = (v - hi.astype(F32)).astype(BF16)
            return carry

        for i in range(first, end):
            a_copy(i).wait()
            lax.fori_loop(i * n, (i + 1) * n, prep, 0, unroll=2)

    prep_chunks(0, CHUNKS // 2)
    table.wait()
    pl.semaphore_wait(barrier, len(greeted))
    for h in both:
        for j in (2, 1, 3):
            ca_copy(h, j).start()
    for l in range(1, LEAD_MAX + 1):
        lag_copy(l).start()
    prep_chunks(CHUNKS // 2, CHUNKS)

    def products(h, src, o_src, o_prev, forward, between=None, at=48):
        def pair(p, carry):
            ts = (2 * p, 2 * p + 1)
            rows = []
            for t in ts:
                rows += split(src[tab[o_src, t]])
            lhs = jnp.concatenate(rows, axis=0).astype(BF16)
            lhs = jnp.concatenate([lhs, lhs], axis=1)
            tiles = wf if forward else wt
            (h1, l1), (h2, l2) = [(tiles[t, 0], tiles[t, 1]) for t in ts]
            w = jnp.concatenate(
                [jnp.concatenate([h1, h2], axis=1), jnp.concatenate([l1, l2], axis=1)], axis=0
            )
            out = lax.dot_general(lhs, w, (((1,), (0,)), ((), ())), preferred_element_type=F32)
            for i, t in enumerate(ts):
                row, lanes = 16 * i, slice(i * T, (i + 1) * T)
                s_buf[h][t] = out[row:row + 8, lanes] + out[row + 8:row + 16, lanes] + s_buf[h][tab[o_prev, t]]
            return carry

        if between:
            lax.fori_loop(0, at, pair, 0, unroll=16)
            between()
            lax.fori_loop(at, NT // 2, pair, 0, unroll=16)
        else:
            lax.fori_loop(0, NT // 2, pair, 0, unroll=32)

    def place(h, c, g, stat):
        if c == 0:
            pb[h, c, g, 0] = stat

        def one(i, carry):
            pb[h, c, g, 1 + i] = s_buf[h][tab[LAST_COL + c, g * 32 + i]]
            return carry

        lax.fori_loop(0, 32, one, 0, unroll=16)

    def start_ring(h, stat):
        for which, copies in ((3, (0, 1)), (1, (2,)), (2, (3,)), (0, ())):
            for c in range(2):
                place(h, c, ring(c)[which], stat)
                for i in copies:
                    rz_copy(h, c, i).start()

    def relay_ring(h):
        for c in range(2):
            g, up, dn, opp = ring(c)
            for side, block in ((0, up), (1, dn)):
                rz_copy(h, c, side).wait_recv()
                at, n = half_of(c, side)
                here = pl.ds(at, n)
                pb[h, c, block, here] = pb[h, c, block, here] + fb[h, c, side, 0:n]
                rz_copy(h, c, 4 + side).start()

    def start_plane(h):
        for c in range(2):
            for i in (2, 3, 4, 5):
                rz_copy(h, c, i).wait_recv()

            def ring_sum(i):
                return pb[h, c, g_of[c], i] + rb[h, c, 0, i] + rb[h, c, 1, i]

            for m in range(8):
                for k in range(4):
                    qb[h, c, m, 1 + k] = ring_sum(1 + m * 4 + k)
            if c == 0:
                stat = ring_sum(0)
                for m in range(8):
                    qb[h, c, m, 0] = stat
            for j in (4, 3, 5, 2, 6, 1, 7):
                rp_copy(h, c, j).start()

    def new_weight(old, sums, at):
        psq, dsq = [
            jnp.sum(jnp.where(lane == at + e, sums, 0.0), axis=1, keepdims=True) for e in range(2)
        ]
        return jnp.sqrt(old * jnp.sqrt((psq + epsilon) / (dsq + epsilon)))

    def lanes_sum(v):
        return jnp.sum(v, axis=1, keepdims=True)

    def update(h, it):
        square = zero
        for c in range(2):
            m = m_of[c]
            for j in range(1, 8):
                rp_copy(h, c, j).wait_recv()

            def total(k):
                return qb[h, c, m, k] + sum(tb[h, c, j, k] for j in range(7))

            if c == 0:
                old = wgt[h]
                wgt[h] = jnp.where(it > 0, new_weight(old, total(0), 0), old)
            pstep = step_scale / wgt[h]
            for kk in range(4):
                k = c * 4 + kk
                primal = pr[h, k]
                new = jnp.maximum(primal - pstep * (cost[k:k + 1, :] - total(1 + kk)), 0.0)
                change = new - primal
                square = square + change * change
                pr[h, k] = new
                xg[h][c * 128 + g_of[c] * 32 + m * 4 + kk] = 2.0 * new - primal
            for j in (4, 3, 5, 2, 6, 1, 7):
                ap_copy(h, c, j).start()
        yb[h, 1 - core, 16] = square
        yb[h, core, 16] = square

    def start_spread(h):
        for c in range(2):
            for j in range(1, 8):
                ap_copy(h, c, j, True).wait_recv()
            for i in range(4):
                az_copy(h, c, i).start()

    def relay_spread(h):
        for c in range(2):
            for i in range(2):
                az_copy(h, c, i, True).wait_recv()
                az_copy(h, c, 4 + i).start()

    def transposed(h, between=None):
        products(h, dg[h], ROW, PREV_COL, False, between)
        start_ring(h, jnp.where(lane == 0, dg[h][16], dg[h][16] + dg[h][33]))

    def send_sums(h, it):
        terms_copy(h).wait_recv()
        ych[h] = yb[h, core] + yc[h]
        sums_copy(h, it).start()

    def dual_update(h, it):
        @pl.when(it == 0)
        def _():
            rhs_copy(h, True).wait_recv()
            rhs_copy(h).wait_send()
            for j in range(1, 4):
                ca_copy(h, j).wait_send()

        @pl.when(it > 0)
        def _():
            prices_copy(h).wait_send()

        sums_copy(h, it).wait_recv()
        dstep = step_scale * wgt[h]
        square = zero
        for k in range(16):
            push = ych[h, k] + yx[h, it, k]
            old = dg[h][core * 17 + k]
            new = old + dstep * (rhs[h, k] - push)
            change = new - old
            square = square + change * change
            dg[h][core * 17 + k] = new
        primal_square = lanes_sum(ych[h, 16] + yx[h, it, 16])
        dg[h][core * 17 + 16] = jnp.where(
            lane == 0, primal_square, jnp.where(lane == 1, lanes_sum(square), 0.0)
        )

    def turn(t, carry):
        v = af[t].T
        hi = v.astype(BF16)
        wf[t, 0] = hi
        wf[t, 1] = (v - hi.astype(F32)).astype(BF16)
        return carry

    def turn_some(it, first, end):
        @pl.when(it == 0)
        def _():
            lax.fori_loop(first, end, turn, 0, unroll=2)

    def iteration(it, carry):
        @pl.when(it == 0)
        def _():
            for j in range(1, 4):
                ca_recv(1, j).wait_recv()

        @pl.when(it > 0)
        def _():
            prices_copy(1, True).wait_recv()

        transposed(1)
        for h in both:
            relay_ring(h)

        turn_some(it, 0, 40)
        for h in both:
            start_plane(h)
        turn_some(it, 40, 88)
        for h in both:
            update(h, it)
        turn_some(it, 88, NT)
        for h in both:
            start_spread(h)
        for h in both:
            relay_spread(h)

        @pl.when(it == 0)
        def _():
            for l in range(1, LEAD_MAX + 1):
                lag_copy(l).wait_recv()
            for h in both:
                rows = slice(8 * h, 8 * h + 8)
                for k in range(8):
                    lanes = slice(k * T, (k + 1) * T)
                    periods = jnp.broadcast_to(lead[k:k + 1, :], (8, T))
                    lagged = jnp.zeros((8, T), F32)
                    for l in range(1, LEAD_MAX + 1):
                        lagged = jnp.where(periods == l, lag[l - 1, rows, lanes], lagged)
                    rhs[h, chip * 8 + k] = dem[rows, lanes] - return_share * lagged
                rhs_copy(h).start()
            for l in range(1, LEAD_MAX + 1):
                lag_copy(l).wait_send()

        for h in both:
            for c in range(2):
                for i in (2, 3, 4, 5):
                    az_copy(h, c, i, True).wait_recv()
            products(h, xg[h], COL, PREV_ROW, True, (lambda: send_sums(0, it)) if h else None)
            for r in range(RT):
                yb[h, r // 8 % 2, r // 16 * 8 + r % 8] = s_buf[h][tab[LAST_ROW, r]]
            terms_copy(h).start()
        send_sums(1, it)
        for h in both:
            for c in range(2):
                for i in range(6):
                    rz_copy(h, c, i).wait_send()
                    az_copy(h, c, i).wait_send()
                for j in range(1, 8):
                    rp_copy(h, c, j).wait_send()
                    ap_copy(h, c, j).wait_send()
            terms_copy(h).wait_send()
        dual_update(0, it)

        @pl.when(it < ITERS - 1)
        def _():
            prices_copy(0).start()
            prices_copy(0, True).wait_recv()

            def other_half():
                dual_update(1, it)
                prices_copy(1).start()

            transposed(0, other_half)

        @pl.when(it == ITERS - 1)
        def _():
            dual_update(1, it)

        for h in both:
            sums_copy(h, it).wait_send()
        return carry

    for j in range(1, 4):
        ca_recv(0, j).wait_recv()
    transposed(0)
    lax.fori_loop(0, ITERS, iteration, 0)

    packed = zero
    for h in both:
        stat = dg[h][core * 17 + 16]
        for e in range(2):
            value = lanes_sum(jnp.where(lane == e, stat, 0.0))
            packed = jnp.where(lane == 2 * h + e, value, packed)
    fs[0] = packed
    first = rc(fs.at[0], fc, fi_s.at[31], fi_r.at[31], b, other_core)
    first.start()
    for h in both:
        for k in range(8):
            prim_out[8 * h:8 * h + 8, k * T:(k + 1) * T] = pr[h, k]
            dual_out[8 * h:8 * h + 8, k * T:(k + 1) * T] = dg[h][core * 17 + chip * 8 + k]
    first.wait_recv()
    fs[1] = jnp.where(lane % 2 == 0, packed, packed + fc[...])
    copies = [rc(fs.at[1], fa.at[i], fi_s.at[i], fi_r.at[i], *to) for i, to in enumerate(band)]
    for c in copies:
        c.start()
    for c in copies:
        c.wait_recv()
    sums = fs[1] + jnp.sum(fa[...], axis=0)
    for h in both:
        w_out[8 * h:8 * h + 8, :] = new_weight(wgt[h], sums, 2 * h)
    first.wait_send()
    for c in copies:
        c.wait_send()


def on_device(
    demand, lead_periods, matrix_tiles, tile_pos, cost_vector, primal_init, dual_init, weight_init
):
    vmem = pl.BlockSpec(memory_space=pltpu.VMEM)
    smem = pl.BlockSpec(memory_space=pltpu.SMEM)
    hbm = pl.BlockSpec(memory_space=pl.ANY)
    dma = pltpu.SemaphoreType.DMA

    def buf(*shape, dtype=F32):
        return pltpu.VMEM(shape, dtype)

    primal, dual, weight = pl.pallas_call(
        kernel,
        out_shape=(
            jax.ShapeDtypeStruct((16, 1024), F32),
            jax.ShapeDtypeStruct((16, 1024), F32),
            jax.ShapeDtypeStruct((16, T), F32),
        ),
        in_specs=[smem] + [hbm] * 7,
        out_specs=(vmem, vmem, vmem),
        scratch_shapes=[
            pltpu.SMEM((8, NT), jnp.int32),
            buf(8, NT, dtype=jnp.int32),
            buf(1, NT, dtype=jnp.int32),
            buf(16, 1024),
            buf(8, T, dtype=jnp.int32),
            buf(8, T),
            buf(16, 1024),
            buf(16, 1024),
            buf(NT, T, T),
            buf(NT, 2, T, T, dtype=BF16),
            buf(NT, 2, T, T, dtype=BF16),
            buf(NT + 1, 8, T),
            buf(NT + 1, 8, T),
            buf(CT, 8, T),
            buf(CT, 8, T),
            buf(2, 2, 4, 33, 8, T),
            buf(2, 2, 2, 17, 8, T),
            buf(2, 2, 2, 33, 8, T),
            buf(2, 2, 8, 5, 8, T),
            buf(2, 2, 7, 5, 8, T),
            buf(34, 8, T),
            buf(34, 8, T),
            buf(2, 2, 17, 8, T),
            buf(2, 17, 8, T),
            buf(2, 17, 8, T),
            buf(2, ITERS, 17, 8, T),
            buf(2, 8, 8, T),
            buf(2, 16, 8, T),
            buf(4, 16, 1024),
            buf(2, 8, T),
            buf(2, 8, T),
            buf(8, T),
            buf(31, 8, T),
            dma((7,)), dma((CHUNKS,)), dma((4,)), dma((4,)),
            dma((2, 3)), dma((2, 3)), dma((2, 2, 6)), dma((2, 2, 6)), dma((2, 2, 7)), dma((2, 2, 7)),
            dma((2, 2, 7)), dma((2, 2, 7)), dma((2, 2, 6)), dma((2, 2, 6)), dma((3, 2)), dma((3, 2)),
            dma((2, ITERS)), dma((2,)), dma((2,)), dma((32,)), dma((32,)),
        ],
        compiler_params=pltpu.CompilerParams(
            collective_id=0, has_side_effects=True, vmem_limit_bytes=60 * 2**20
        ),
    )(
        weight_init,
        tile_pos.reshape(1, NT),
        demand.T,
        lead_periods.reshape(8, T),
        matrix_tiles.reshape(NT, T, T),
        cost_vector.reshape(8, T),
        primal_init.T,
        dual_init.T,
    )
    return primal.T, dual.T, weight[:, 0]


def solution(mesh):
    in_specs = (
        P(("band", "col"), None),
        P(("band", "col")),
        P("band", "col", None, None, None),
        P("band", "col", None),
        P(("band", "col")),
        P(("band", "col"), None),
        P(("band", "col"), None),
        P(),
    )
    out_specs = (P(("band", "col"), None), P(("band", "col"), None), P())
    return jax.shard_map(
        on_device, mesh=mesh, in_specs=in_specs, out_specs=out_specs, check_vma=False
    )
```

```python
import jax
import jax.numpy as jnp
from jax import lax
from jax.experimental import pallas as pl
from jax.experimental.pallas import tpu as pltpu
from jax.sharding import PartitionSpec as P

ITERS = 3
LEAD_MAX = 4
step_scale = 0.45
return_share = 0.6
epsilon = 1e-06

NT = 128
T = 128
CT = 256
RT = 32
F32 = jnp.float32
BF16 = jnp.bfloat16
CHUNKS = 16
MESH = pl.DeviceIdType.MESH

ROW, COL, PREV_COL, PREV_ROW, LAST_COL, LAST_ROW = 0, 1, 2, 3, 4, 6


def index_table(pos):
    shift = lax.shift_right_logical
    here = jnp.broadcast_to(pos, (NT, NT))
    above = here.T
    u = lax.broadcasted_iota(jnp.int32, (NT, NT), 0)
    t = lax.broadcasted_iota(jnp.int32, (NT, NT), 1)

    def row(v):
        return shift(v, 8)

    def col(v):
        return v & 255

    def row_place(v):
        r = row(v)
        return (shift(r, 3) & 1) * 17 + shift(r, 4) * 8 + (r & 7)

    def col_place(v):
        k, z, x, y = v & 7, shift(v, 3) & 3, shift(v, 5) & 1, shift(col(v), 6)
        kk = k & 3
        return jnp.where(k < 4, z * 32 + y * 8 + x * 4 + kk, 128 + y * 32 + z * 8 + x * 4 + kk)

    def latest(where):
        found = jnp.max(jnp.where(where, u, -1), axis=0, keepdims=True)
        return jnp.where(found < 0, NT, found)

    place = col_place(above)
    return [
        row_place(pos),
        col_place(pos),
        latest((col(above) == col(here)) & (u < t)),
        latest((row(above) == row(here)) & (u < t)),
        latest(place == t),
        latest(place == t + NT),
        latest(row(above) == t),
    ]


def split(v):
    hi = v.astype(BF16).astype(F32)
    return hi, v - hi


def kernel(
    w0, pos_in, dem_in, lead_in, a_hbm, cost_in, prim_in, dual_in,
    prim_out, dual_out, w_out,
    tab, tab_v, pos, dem, lead, cost, prim0, dual0,
    af, wt, wf, s0, s1, xg0, xg1, pb, fb, rb, qb, tb, dg0, dg1, yb, yc, ych, yx, pr, rhs, lag, wgt, fs, fc, fa,
    in_sem, a_sem, lag_s, lag_r, ca_s, ca_r, rz_s, rz_r, rp_s, rp_r, ap_s, ap_r, az_s, az_r, col_s, col_r,
    sums_r, rh_s, rh_r, fi_s, fi_r,
):
    b = lax.axis_index("band")
    q = lax.axis_index("col")
    y, x, z = b // 8, (b // 4) % 2, b % 4
    xg, dg, s_buf = (xg0, xg1), (dg0, dg1), (s0, s1)
    both = range(2)

    def rc(src, dst, ss, rs, band, col):
        return pltpu.make_async_remote_copy(
            src_ref=src, dst_ref=dst, send_sem=ss, recv_sem=rs,
            device_id=(band, col), device_id_type=MESH,
        )

    g_of = (z, y)
    m_of = (y * 2 + x, z * 2 + x)

    def band_of(c, g, m):
        o, xx = m // 2, m % 2
        return o * 8 + xx * 4 + g if c == 0 else g * 8 + xx * 4 + o

    band = [((b + i) % 32, q) for i in range(1, 32)]
    core, chip = q % 2, q // 2
    other_core, other_chip = q + 1 - 2 * core, (q + 2) % 4

    def a_copy(i):
        n = NT // CHUNKS
        return pltpu.make_async_copy(a_hbm.at[pl.ds(i * n, n)], af.at[pl.ds(i * n, n)], a_sem.at[i])

    def lag_copy(l):
        return rc(dem, lag.at[l - 1], lag_s.at[l - 1], lag_r.at[l - 1], (b + l) % 32, q)

    def ca_copy(h, j):
        own = dg[h].at[pl.ds(core * 17 + chip * 8, 8)]
        return rc(own, own, ca_s.at[h, j - 1], ca_r.at[h, j - 1], b, (q + j) % 4)

    def ca_recv(h, j):
        q2 = (q + 4 - j) % 4
        slot = dg[h].at[pl.ds(q2 % 2 * 17 + q2 // 2 * 8, 8)]
        return rc(slot, slot, ca_s.at[h, j - 1], ca_r.at[h, j - 1], b, q2)

    def terms_copy(h):
        return rc(yb.at[h, 1 - core], yc.at[h], col_s.at[0, h], col_r.at[0, h], b, other_core)

    def sums_copy(h, it):
        return rc(ych.at[h], yx.at[h, it], col_s.at[1, h], sums_r.at[h, it], b, other_chip)

    def prices_copy(h, back=False):
        slot = dg[h].at[pl.ds((1 - core if back else core) * 17, 17)]
        return rc(slot, slot, col_s.at[2, h], col_r.at[2, h], b, other_core)

    def rhs_copy(h, back=False):
        slot = rhs.at[h, pl.ds((1 - chip if back else chip) * 8, 8)]
        return rc(slot, slot, rh_s.at[h], rh_r.at[h], b, other_chip)

    def ring(c):
        g = g_of[c]
        return g, (g + 1) % 4, (g + 3) % 4, (g + 2) % 4

    def half_of(c, half):
        return (17, 16) if half else (c, 17 - c)

    def rz_copy(h, c, i):
        g, up, dn, opp = ring(c)
        block, side, half = ((opp, 0, 0), (opp, 1, 1), (up, 0, 1), (dn, 1, 0), (up, 0, 0), (dn, 1, 1))[i]
        at, n = half_of(c, half)
        src = pb.at[h, c, block, pl.ds(at, n)]
        dst = fb.at[h, c, side, pl.ds(0, n)] if i < 2 else rb.at[h, c, side, pl.ds(at, n)]
        return rc(
            src, dst, rz_s.at[h, c, i], rz_r.at[h, c, i], band_of(c, dn if side else up, m_of[c]), q
        )

    def rp_copy(h, c, j):
        m2 = (m_of[c] + j) % 8
        part = pl.ds(1, 4) if c else pl.ds(0, 5)
        return rc(
            qb.at[h, c, m2, part], tb.at[h, c, j - 1, part], rp_s.at[h, c, j - 1], rp_r.at[h, c, j - 1],
            band_of(c, g_of[c], m2), q,
        )

    def ap_copy(h, c, j, back=False):
        m = m_of[c]
        m2 = (m + 8 - j) % 8 if back else (m + j) % 8
        slot = xg[h].at[pl.ds(c * 128 + g_of[c] * 32 + (m2 if back else m) * 4, 4)]
        return rc(slot, slot, ap_s.at[h, c, j - 1], ap_r.at[h, c, j - 1], band_of(c, g_of[c], m2), q)

    def az_copy(h, c, i, back=False):
        g, up, dn, opp = ring(c)
        lo, hi = (dn, up) if back else (g, g)
        block, half = (
            (lo, 0), (hi, 1), (lo, 1), (hi, 0), (opp if back else dn, 0), (opp if back else up, 1)
        )[i]
        slot = xg[h].at[pl.ds(c * 128 + block * 32 + half * 16, 16)]
        to = band_of(c, dn if i % 2 else up, m_of[c])
        return rc(slot, slot, az_s.at[h, c, i], az_r.at[h, c, i], to, q)

    inputs = [
        pltpu.make_async_copy(src, dst, in_sem.at[i])
        for i, (src, dst) in enumerate(
            ((pos_in, pos), (dual_in, dual0), (dem_in, dem), (prim_in, prim0), (cost_in, cost), (lead_in, lead))
        )
    ]
    for c in inputs:
        c.start()
    for i in range(CHUNKS):
        a_copy(i).start()
    greeted = band + [(b, (q + j) % 4) for j in (1, 2, 3)]
    barrier = pltpu.get_barrier_semaphore()
    for to in greeted:
        pl.semaphore_signal(barrier, inc=1, device_id=to, device_id_type=MESH)
    zero = jnp.zeros((8, T), F32)
    sublane = lax.broadcasted_iota(jnp.int32, (8, T), 0)
    lane = lax.broadcasted_iota(jnp.int32, (8, T), 1)
    for c in inputs:
        c.wait()
    for h in both:
        for k in range(8):
            dg[h][core * 17 + chip * 8 + k] = dual0[8 * h:8 * h + 8, k * T:(k + 1) * T]
            pr[h, k] = prim0[8 * h:8 * h + 8, k * T:(k + 1) * T]
        dg[h][16] = zero
        dg[h][33] = zero
        weight = zero
        for i in range(8):
            weight = jnp.where(sublane == i, w0[8 * h + i], weight)
        wgt[h] = weight
        s_buf[h][NT] = zero

    tab_v[...] = jnp.zeros((8, NT), jnp.int32)
    for i, entry in enumerate(index_table(pos[...])):
        tab_v[i:i + 1, :] = entry
    table = pltpu.make_async_copy(tab_v, tab, in_sem.at[6])
    table.start()

    def prep_chunks(first, end):
        n = NT // CHUNKS

        def prep(t, carry):
            v = af[t]
            hi = v.astype(BF16)
            wt[t, 0] = hi
            wt[t, 1] = (v - hi.astype(F32)).astype(BF16)
            return carry

        for i in range(first, end):
            a_copy(i).wait()
            lax.fori_loop(i * n, (i + 1) * n, prep, 0, unroll=2)

    prep_chunks(0, CHUNKS // 2)
    table.wait()
    pl.semaphore_wait(barrier, len(greeted))
    for h in both:
        for j in (2, 1, 3):
            ca_copy(h, j).start()
    prep_chunks(CHUNKS // 2, CHUNKS)

    def products(h, src, o_src, o_prev, forward, between=None, at=48):
        def pair(p, carry):
            ts = (2 * p, 2 * p + 1)
            rows = []
            for t in ts:
                rows += split(src[tab[o_src, t]])
            lhs = jnp.concatenate(rows, axis=0).astype(BF16)
            lhs = jnp.concatenate([lhs, lhs], axis=1)
            tiles = wf if forward else wt
            (h1, l1), (h2, l2) = [(tiles[t, 0], tiles[t, 1]) for t in ts]
            w = jnp.concatenate(
                [jnp.concatenate([h1, h2], axis=1), jnp.concatenate([l1, l2], axis=1)], axis=0
            )
            out = lax.dot_general(lhs, w, (((1,), (0,)), ((), ())), preferred_element_type=F32)
            for i, t in enumerate(ts):
                row, lanes = 16 * i, slice(i * T, (i + 1) * T)
                s_buf[h][t] = out[row:row + 8, lanes] + out[row + 8:row + 16, lanes] + s_buf[h][tab[o_prev, t]]
            return carry

        if between:
            lax.fori_loop(0, at, pair, 0, unroll=16)
            between()
            lax.fori_loop(at, NT // 2, pair, 0, unroll=16)
        else:
            lax.fori_loop(0, NT // 2, pair, 0, unroll=32)

    def place(h, c, g, stat):
        if c == 0:
            pb[h, c, g, 0] = stat

        def one(i, carry):
            pb[h, c, g, 1 + i] = s_buf[h][tab[LAST_COL + c, g * 32 + i]]
            return carry

        lax.fori_loop(0, 32, one, 0, unroll=16)

    def start_ring(h, stat):
        for which, copies in ((3, (0, 1)), (1, (2,)), (2, (3,)), (0, ())):
            for c in range(2):
                place(h, c, ring(c)[which], stat)
                for i in copies:
                    rz_copy(h, c, i).start()

    def relay_ring(h):
        for c in range(2):
            g, up, dn, opp = ring(c)
            for side, block in ((0, up), (1, dn)):
                rz_copy(h, c, side).wait_recv()
                at, n = half_of(c, side)
                here = pl.ds(at, n)
                pb[h, c, block, here] = pb[h, c, block, here] + fb[h, c, side, 0:n]
                rz_copy(h, c, 4 + side).start()

    def start_plane(h):
        for c in range(2):
            for i in (2, 3, 4, 5):
                rz_copy(h, c, i).wait_recv()

            def ring_sum(i):
                return pb[h, c, g_of[c], i] + rb[h, c, 0, i] + rb[h, c, 1, i]

            for m in range(8):
                for k in range(4):
                    qb[h, c, m, 1 + k] = ring_sum(1 + m * 4 + k)
            if c == 0:
                stat = ring_sum(0)
                for m in range(8):
                    qb[h, c, m, 0] = stat
            for j in (4, 3, 5, 2, 6, 1, 7):
                rp_copy(h, c, j).start()

    def new_weight(old, sums, at):
        psq, dsq = [
            jnp.sum(jnp.where(lane == at + e, sums, 0.0), axis=1, keepdims=True) for e in range(2)
        ]
        return jnp.sqrt(old * jnp.sqrt((psq + epsilon) / (dsq + epsilon)))

    def lanes_sum(v):
        return jnp.sum(v, axis=1, keepdims=True)

    def update(h, it):
        square = zero
        for c in range(2):
            m = m_of[c]
            for j in range(1, 8):
                rp_copy(h, c, j).wait_recv()

            def total(k):
                return qb[h, c, m, k] + sum(tb[h, c, j, k] for j in range(7))

            if c == 0:
                old = wgt[h]
                wgt[h] = jnp.where(it > 0, new_weight(old, total(0), 0), old)
            pstep = step_scale / wgt[h]
            for kk in range(4):
                k = c * 4 + kk
                primal = pr[h, k]
                new = jnp.maximum(primal - pstep * (cost[k:k + 1, :] - total(1 + kk)), 0.0)
                change = new - primal
                square = square + change * change
                pr[h, k] = new
                xg[h][c * 128 + g_of[c] * 32 + m * 4 + kk] = 2.0 * new - primal
            for j in (4, 3, 5, 2, 6, 1, 7):
                ap_copy(h, c, j).start()
        yb[h, 1 - core, 16] = square
        yb[h, core, 16] = square

    def start_spread(h):
        for c in range(2):
            for j in range(1, 8):
                ap_copy(h, c, j, True).wait_recv()
            for i in range(4):
                az_copy(h, c, i).start()

    def relay_spread(h):
        for c in range(2):
            for i in range(2):
                az_copy(h, c, i, True).wait_recv()
                az_copy(h, c, 4 + i).start()

    def transposed(h, between=None):
        products(h, dg[h], ROW, PREV_COL, False, between)
        start_ring(h, jnp.where(lane == 0, dg[h][16], dg[h][16] + dg[h][33]))

    def send_sums(h, it):
        terms_copy(h).wait_recv()
        ych[h] = yb[h, core] + yc[h]
        sums_copy(h, it).start()

    def dual_update(h, it):
        @pl.when(it == 0)
        def _():
            rhs_copy(h, True).wait_recv()
            rhs_copy(h).wait_send()
            for j in range(1, 4):
                ca_copy(h, j).wait_send()

        @pl.when(it > 0)
        def _():
            prices_copy(h).wait_send()

        sums_copy(h, it).wait_recv()
        dstep = step_scale * wgt[h]
        square = zero
        for k in range(16):
            push = ych[h, k] + yx[h, it, k]
            old = dg[h][core * 17 + k]
            new = old + dstep * (rhs[h, k] - push)
            change = new - old
            square = square + change * change
            dg[h][core * 17 + k] = new
        primal_square = lanes_sum(ych[h, 16] + yx[h, it, 16])
        dg[h][core * 17 + 16] = jnp.where(
            lane == 0, primal_square, jnp.where(lane == 1, lanes_sum(square), 0.0)
        )

    def turn(t, carry):
        v = af[t].T
        hi = v.astype(BF16)
        wf[t, 0] = hi
        wf[t, 1] = (v - hi.astype(F32)).astype(BF16)
        return carry

    def turn_some(it, first, end):
        @pl.when(it == 0)
        def _():
            lax.fori_loop(first, end, turn, 0, unroll=2)

    def iteration(it, carry):
        @pl.when(it == 0)
        def _():
            for j in range(1, 4):
                ca_recv(1, j).wait_recv()

        @pl.when(it > 0)
        def _():
            prices_copy(1, True).wait_recv()

        transposed(1)
        for h in both:
            relay_ring(h)

        turn_some(it, 0, 40)
        for h in both:
            start_plane(h)
        @pl.when(it == 0)
        def _():
            for l in range(1, LEAD_MAX + 1):
                lag_copy(l).start()

        turn_some(it, 40, 88)
        for h in both:
            update(h, it)
        turn_some(it, 88, NT)
        for h in both:
            start_spread(h)
        for h in both:
            relay_spread(h)

        @pl.when(it == 0)
        def _():
            for l in range(1, LEAD_MAX + 1):
                lag_copy(l).wait_recv()
            for h in both:
                rows = slice(8 * h, 8 * h + 8)
                for k in range(8):
                    lanes = slice(k * T, (k + 1) * T)
                    periods = jnp.broadcast_to(lead[k:k + 1, :], (8, T))
                    lagged = jnp.zeros((8, T), F32)
                    for l in range(1, LEAD_MAX + 1):
                        lagged = jnp.where(periods == l, lag[l - 1, rows, lanes], lagged)
                    rhs[h, chip * 8 + k] = dem[rows, lanes] - return_share * lagged
                rhs_copy(h).start()
            for l in range(1, LEAD_MAX + 1):
                lag_copy(l).wait_send()

        for h in both:
            for c in range(2):
                for i in (2, 3, 4, 5):
                    az_copy(h, c, i, True).wait_recv()
            products(h, xg[h], COL, PREV_ROW, True, (lambda: send_sums(0, it)) if h else None)
            for r in range(RT):
                yb[h, r // 8 % 2, r // 16 * 8 + r % 8] = s_buf[h][tab[LAST_ROW, r]]
            terms_copy(h).start()
        send_sums(1, it)
        for h in both:
            for c in range(2):
                for i in range(6):
                    rz_copy(h, c, i).wait_send()
                    az_copy(h, c, i).wait_send()
                for j in range(1, 8):
                    rp_copy(h, c, j).wait_send()
                    ap_copy(h, c, j).wait_send()
            terms_copy(h).wait_send()
        dual_update(0, it)

        @pl.when(it < ITERS - 1)
        def _():
            prices_copy(0).start()
            prices_copy(0, True).wait_recv()

            def other_half():
                dual_update(1, it)
                prices_copy(1).start()

            transposed(0, other_half)

        @pl.when(it == ITERS - 1)
        def _():
            dual_update(1, it)

        for h in both:
            sums_copy(h, it).wait_send()
        return carry

    for j in range(1, 4):
        ca_recv(0, j).wait_recv()
    transposed(0)
    lax.fori_loop(0, ITERS, iteration, 0)

    packed = zero
    for h in both:
        stat = dg[h][core * 17 + 16]
        for e in range(2):
            value = lanes_sum(jnp.where(lane == e, stat, 0.0))
            packed = jnp.where(lane == 2 * h + e, value, packed)
    fs[0] = packed
    first = rc(fs.at[0], fc, fi_s.at[31], fi_r.at[31], b, other_core)
    first.start()
    for h in both:
        for k in range(8):
            prim_out[8 * h:8 * h + 8, k * T:(k + 1) * T] = pr[h, k]
            dual_out[8 * h:8 * h + 8, k * T:(k + 1) * T] = dg[h][core * 17 + chip * 8 + k]
    first.wait_recv()
    fs[1] = jnp.where(lane % 2 == 0, packed, packed + fc[...])
    copies = [rc(fs.at[1], fa.at[i], fi_s.at[i], fi_r.at[i], *to) for i, to in enumerate(band)]
    for c in copies:
        c.start()
    for c in copies:
        c.wait_recv()
    sums = fs[1] + jnp.sum(fa[...], axis=0)
    for h in both:
        w_out[8 * h:8 * h + 8, :] = new_weight(wgt[h], sums, 2 * h)
    first.wait_send()
    for c in copies:
        c.wait_send()


def on_device(
    demand, lead_periods, matrix_tiles, tile_pos, cost_vector, primal_init, dual_init, weight_init
):
    vmem = pl.BlockSpec(memory_space=pltpu.VMEM)
    smem = pl.BlockSpec(memory_space=pltpu.SMEM)
    hbm = pl.BlockSpec(memory_space=pl.ANY)
    dma = pltpu.SemaphoreType.DMA

    def buf(*shape, dtype=F32):
        return pltpu.VMEM(shape, dtype)

    primal, dual, weight = pl.pallas_call(
        kernel,
        out_shape=(
            jax.ShapeDtypeStruct((16, 1024), F32),
            jax.ShapeDtypeStruct((16, 1024), F32),
            jax.ShapeDtypeStruct((16, T), F32),
        ),
        in_specs=[smem] + [hbm] * 7,
        out_specs=(vmem, vmem, vmem),
        scratch_shapes=[
            pltpu.SMEM((8, NT), jnp.int32),
            buf(8, NT, dtype=jnp.int32),
            buf(1, NT, dtype=jnp.int32),
            buf(16, 1024),
            buf(8, T, dtype=jnp.int32),
            buf(8, T),
            buf(16, 1024),
            buf(16, 1024),
            buf(NT, T, T),
            buf(NT, 2, T, T, dtype=BF16),
            buf(NT, 2, T, T, dtype=BF16),
            buf(NT + 1, 8, T),
            buf(NT + 1, 8, T),
            buf(CT, 8, T),
            buf(CT, 8, T),
            buf(2, 2, 4, 33, 8, T),
            buf(2, 2, 2, 17, 8, T),
            buf(2, 2, 2, 33, 8, T),
            buf(2, 2, 8, 5, 8, T),
            buf(2, 2, 7, 5, 8, T),
            buf(34, 8, T),
            buf(34, 8, T),
            buf(2, 2, 17, 8, T),
            buf(2, 17, 8, T),
            buf(2, 17, 8, T),
            buf(2, ITERS, 17, 8, T),
            buf(2, 8, 8, T),
            buf(2, 16, 8, T),
            buf(4, 16, 1024),
            buf(2, 8, T),
            buf(2, 8, T),
            buf(8, T),
            buf(31, 8, T),
            dma((7,)), dma((CHUNKS,)), dma((4,)), dma((4,)),
            dma((2, 3)), dma((2, 3)), dma((2, 2, 6)), dma((2, 2, 6)), dma((2, 2, 7)), dma((2, 2, 7)),
            dma((2, 2, 7)), dma((2, 2, 7)), dma((2, 2, 6)), dma((2, 2, 6)), dma((3, 2)), dma((3, 2)),
            dma((2, ITERS)), dma((2,)), dma((2,)), dma((32,)), dma((32,)),
        ],
        compiler_params=pltpu.CompilerParams(
            collective_id=0, has_side_effects=True, vmem_limit_bytes=60 * 2**20
        ),
    )(
        weight_init,
        tile_pos.reshape(1, NT),
        demand.T,
        lead_periods.reshape(8, T),
        matrix_tiles.reshape(NT, T, T),
        cost_vector.reshape(8, T),
        primal_init.T,
        dual_init.T,
    )
    return primal.T, dual.T, weight[:, 0]


def solution(mesh):
    in_specs = (
        P(("band", "col"), None),
        P(("band", "col")),
        P("band", "col", None, None, None),
        P("band", "col", None),
        P(("band", "col")),
        P(("band", "col"), None),
        P(("band", "col"), None),
        P(),
    )
    out_specs = (P(("band", "col"), None), P(("band", "col"), None), P())
    return jax.shard_map(
        on_device, mesh=mesh, in_specs=in_specs, out_specs=out_specs, check_vma=False
    )
```
